512 devices in a mesh: lat: 16 (over x, z_hi, core), lon: 32 (over z_lo, y).
Axes of the slice: x: 4, y: 4, z: 16 (z_hi: 2, z_lo: 8; z = z_hi * 8 + z_lo), core: 2. Of those that a mesh axis runs over, the one named last changes fastest.
Arguments:
- prior_ensemble: bfloat16 [3, 128, 32, 4096], P(None, None, 'lat', 'lon'), may hold values from -6 to 6
- observed: float32 [16, 32, 256], P('lat', 'lon'), may hold values from -6 to 6
- obs_error: float32 [16, 32, 256], P('lat', 'lon'), may hold values from 0.2 to 80
- obs_index: int32 [16, 32, 256], P('lat', 'lon'), may hold values from 0 to 767
- obs_count: int32 [16, 32], P('lat', 'lon'), may hold values from 128 to 256, as said below
Outputs:
- posterior_ensemble: float32 [3, 128, 32, 4096], P(None, None, 'lat', 'lon')
The draws below stay inside these ranges and needn't reach their ends.
Inputs may be any that keep to these rules, and one draw needn't show every extreme that they name: `obs_count`: every tile has between 128 and 256 live slots; some tile has all 256.
All inputs are finite; a program needn't handle non-finite values.
Results may differ from the reference program's by a relative error of at most 0.0003.
Values sent between devices are 32-bit elements; how exact they have to be, the bound alone decides.
No kernel may reach another device: no remote copies, remote signals or barrier semaphores. Data moves between devices by JAX's collectives and lax.ppermute only.
A program may use at most 128 MiB of HBM per device.

```python
import math
import jax
import jax.numpy as jnp
from jax import lax

ENSEMBLE_SIZE = 128
NOBS = 256
CLAT = 2
CLON = 128
NLAT = 32
NLON = 4096
N_LAT = 16
N_LON = 32


def draw_obs_error(key, part):
    tile_key, row_key = jax.random.split(jax.random.fold_in(key, 11))
    tile_scale = jnp.exp(jax.random.uniform(tile_key, (N_LAT, N_LON, 1), jnp.float32, math.log(0.1), math.log(10.0)))
    row_scale = jnp.exp(jax.random.uniform(row_key, (N_LAT, N_LON, NOBS), jnp.float32, 0.0, math.log(4.0)))
    return 2.0 * tile_scale * row_scale


def draw_obs_count(key, part):
    counts = jax.random.randint(jax.random.fold_in(key, 23), (N_LAT, N_LON), NOBS // 2, NOBS + 1)
    counts = counts.at[0, 0].set(NOBS)
    counts = counts.at[N_LAT - 1, N_LON - 1].set(NOBS // 2)
    return counts.astype(jnp.int32)


def place_ends(array, rng, smallest, high):
    place = [jax.random.randint(jax.random.fold_in(rng, axis), (), 0, length) for axis, length in enumerate(array.shape)]
    widest = array.shape.index(max(array.shape))
    neighbour = place[:widest] + [(place[widest] + 1) % array.shape[widest]] + place[widest + 1:]
    return array.at[tuple(place)].set(smallest).at[tuple(neighbour)].set(high)


def level_of(stream_key, dims, cuts, smallest, top_value):
    loudness, own = 1.0, jax.random.fold_in(stream_key, 6)
    for axis_at, shards_of in cuts:
        steps = jnp.exp(jax.random.uniform(jax.random.fold_in(own, axis_at), (shards_of,), jnp.float32, smallest / len(cuts), top_value / len(cuts)))
        loudness = loudness * jnp.repeat(steps, dims[axis_at] // shards_of).reshape([-1 if axis == axis_at else 1 for axis in range(len(dims))])
    return loudness


def scatter_about(rng, shape, width, limit, shards=(), kind=jnp.bfloat16):
    array = jax.random.normal(rng, shape, jnp.float32) * width
    if len(shards) > 0:
        array = level_of(rng, shape, shards, -0.22, 0.18) * array
    return jnp.clip(array, min=-limit, max=limit).astype(kind)


def setup_inputs(seed: int = 0) -> dict:
    key_list = jax.random.split(jax.random.key(seed), 6)
    prior_ensemble = scatter_about(key_list[0], (3, ENSEMBLE_SIZE, NLAT, NLON), 1.0, 6.0, ((2, 16), (3, 32)))
    observed = scatter_about(key_list[1], (N_LAT, N_LON, NOBS), 1.0, 6.0, ((0, 16), (1, 32)), jnp.float32)
    obs_error = draw_obs_error(jax.random.fold_in(key_list[5], 71), 0)
    obs_index = place_ends(jax.random.randint(key_list[3], (N_LAT, N_LON, NOBS), 0, 3 * CLAT * CLON), jax.random.fold_in(key_list[3], 1), 0, (3 * CLAT * CLON) - 1).astype(jnp.int32)
    obs_count = draw_obs_count(jax.random.fold_in(key_list[5], 71), 0)
    return {"prior_ensemble": prior_ensemble, "observed": observed, "obs_error": obs_error, "obs_index": obs_index, "obs_count": obs_count}


HALF_COURANT = 0.4
ROTATION = 0.8
BAND = math.pi / 6.0

def rotation_rows(first_row, count, total_rows):
    rows = first_row + jnp.arange(count, dtype=jnp.int32)
    latitude = BAND * (2.0 * (rows.astype(jnp.float32) + 0.5) / total_rows - 1.0)
    return (ROTATION * jnp.sin(latitude))[:, None]

def tendency(padded, rotation):
    height, zonal_wind, merid_wind = (padded[0], padded[1], padded[2])
    d_height = -HALF_COURANT * (zonal_wind[..., 1:-1, 2:] - zonal_wind[..., 1:-1, :-2] + (merid_wind[..., 2:, 1:-1] - merid_wind[..., :-2, 1:-1]))
    d_zonal = -HALF_COURANT * (height[..., 1:-1, 2:] - height[..., 1:-1, :-2]) + rotation * merid_wind[..., 1:-1, 1:-1]
    d_merid = -HALF_COURANT * (height[..., 2:, 1:-1] - height[..., :-2, 1:-1]) - rotation * zonal_wind[..., 1:-1, 1:-1]
    return jnp.stack([d_height, d_zonal, d_merid], axis=0)

def wrap_pad(system_vector):
    padded = jnp.pad(system_vector, ((0, 0), (1, 1), (0, 0)))
    return jnp.concatenate([padded[..., -1:], padded, padded[..., :1]], axis=-1)

def reference(prior_ensemble, observed, obs_error, obs_index, obs_count):
    total_rows = CLAT * N_LAT
    rotation = rotation_rows(0, total_rows, total_rows)

    def advance_time(member):
        system_vector = member.astype(jnp.float32)
        upper_coefficient = tendency(wrap_pad(system_vector), rotation)
        midpoint = system_vector + upper_coefficient
        lower_coefficient = tendency(wrap_pad(midpoint), rotation)
        return system_vector + 0.5 * (upper_coefficient + lower_coefficient)
    predicted_ensemble = jnp.moveaxis(lax.map(advance_time, jnp.moveaxis(prior_ensemble, 1, 0)), 0, 1)
    mesh_points = CLAT * CLON
    tile_lat = jnp.arange(N_LAT, dtype=jnp.int32)[:, None, None]
    tile_lon = jnp.arange(N_LON, dtype=jnp.int32)[None, :, None]
    variable_slot = obs_index // mesh_points
    cell_index = obs_index % mesh_points
    latitude_slot = tile_lat * CLAT + cell_index // CLON
    longitude_slot = tile_lon * CLON + cell_index % CLON
    measured_vector = predicted_ensemble[variable_slot, :, latitude_slot, longitude_slot]
    state_mean = lax.optimization_barrier(jnp.mean(measured_vector, axis=-1))
    live = (jnp.arange(NOBS, dtype=jnp.int32)[None, None, :] < obs_count[:, :, None]).astype(jnp.float32)
    weight_rows = live / obs_error
    scaled = ((measured_vector - state_mean[..., None]) * weight_rows[..., None]).reshape(-1, ENSEMBLE_SIZE)
    innovation = ((observed - state_mean) * weight_rows).reshape(-1)
    gram = jnp.dot(scaled.T, scaled, precision=lax.Precision.HIGHEST)
    push = jnp.dot(innovation, scaled, precision=lax.Precision.HIGHEST)
    identity = jnp.eye(ENSEMBLE_SIZE, dtype=jnp.float32)
    prior = float(ENSEMBLE_SIZE - 1)
    factor = jnp.linalg.cholesky(prior * identity + gram)
    inverse = lax.linalg.triangular_solve(factor, identity, left_side=True, lower=True)
    transform = math.sqrt(prior) * inverse.T
    forward = lax.linalg.triangular_solve(factor, push[:, None], left_side=True, lower=True)
    mean_weights = lax.linalg.triangular_solve(factor, forward, left_side=True, lower=True, transpose_a=True)
    weights = transform + mean_weights
    unrolled_vector = predicted_ensemble.reshape(3, ENSEMBLE_SIZE, -1)
    state_center = lax.optimization_barrier(jnp.mean(unrolled_vector, axis=1, keepdims=True))
    anomaly = unrolled_vector - state_center
    posterior_ensemble = state_center + jnp.einsum('fic,ij->fjc', anomaly, weights, precision=lax.Precision.HIGHEST)
    return posterior_ensemble.reshape(predicted_ensemble.shape)
```

```python
import math

import jax
import jax.numpy as jnp
from jax import lax
from jax.sharding import Mesh, PartitionSpec as P

HALF_COURANT = 0.4
ROTATION = 0.8
BAND = math.pi / 6.0
LAT = ("x", "zh", "core")
LON = ("zl", "y")
PLANE = ("x", "core", "y")
LINE = ("zh", "zl")


def rotation_at(rows, total_rows):
    latitude = BAND * (2.0 * (rows.astype(jnp.float32) + 0.5) / total_rows - 1.0)
    return ROTATION * jnp.sin(latitude)


def pair_perms(count, periodic):
    inner = [(i, i ^ 1) for i in range(count)]
    outer = []
    for i in range(1, count, 2):
        if i + 1 < count or periodic:
            j = (i + 1) % count
            outer += [(i, j), (j, i)]
    return inner, outer


def swap(low, high, index, axis, perms):
    even = lax.rem(index, 2) == 0
    inner_perm, outer_perm = perms
    outer = lax.ppermute(jnp.where(even, low, high), axis, outer_perm)
    inner = lax.ppermute(jnp.where(even, high, low), axis, inner_perm)
    return jnp.where(even, outer, inner), jnp.where(even, inner, outer)


def all_sum(block):
    plane = lax.axis_size(PLANE)
    line = lax.axis_size(LINE)
    rows, cols = block.shape
    part = rows // plane
    mine = lax.all_to_all(block.reshape(plane, part, cols), PLANE, 0, 0, tiled=True).sum(0)
    mine = lax.all_to_all(
        jnp.broadcast_to(mine[None], (line, part, cols)), LINE, 0, 0, tiled=True
    ).sum(0)
    whole = lax.all_to_all(
        jnp.broadcast_to(mine[None], (plane, part, cols)), PLANE, 0, 0, tiled=True
    )
    return whole.reshape(rows, cols)


def shards(prior_ensemble, observed, obs_error, obs_index, obs_count):
    a = HALF_COURANT
    state = prior_ensemble.astype(jnp.float32)
    members, rows, cols = state.shape[1:]
    lat_index, lon_index = lax.axis_index(LAT), lax.axis_index(LON)
    lat_count, lon_count = lax.axis_size(LAT), lax.axis_size(LON)
    lat_perms = pair_perms(lat_count, False)
    lon_perms = pair_perms(lon_count, True)
    total_rows = rows * lat_count
    f = rotation_at(lat_index * rows - 1 + jnp.arange(4, dtype=jnp.int32), total_rows)
    has_south = (lat_index > 0).astype(jnp.float32)
    has_north = (lat_index < lat_count - 1).astype(jnp.float32)

    h, u, v = state[0], state[1], state[2]
    zero = jnp.zeros((members, 1), jnp.float32)

    def slope(row):
        row = jnp.concatenate([zero, row, zero], axis=1)
        return row[:, 2:] - row[:, :-2]

    down = jnp.stack([
        h[:, 0], v[:, 0],
        h[:, 0] - a * slope(u[:, 0]) - a * v[:, 1],
        v[:, 0] - a * h[:, 1] - f[1] * u[:, 0],
    ])
    up = jnp.stack([
        h[:, 1], v[:, 1],
        h[:, 1] - a * slope(u[:, 1]) + a * v[:, 0],
        v[:, 1] + a * h[:, 0] - f[2] * u[:, 1],
    ])
    south, north = swap(down, up, lat_index, LAT, lat_perms)

    edge = jnp.transpose(state, (0, 2, 3, 1))
    west, east = swap(edge[:, :, :2], edge[:, :, -2:], lon_index, LON, lon_perms)

    def corner(row):
        return jnp.stack([west[1, row, 1], east[1, row, 0], west[2, row, 1], east[2, row, 0]])

    south_corner, north_corner = swap(corner(0), corner(1), lat_index, LAT, lat_perms)

    west_t = jnp.transpose(west, (0, 3, 1, 2))
    east_t = jnp.transpose(east, (0, 3, 1, 2))
    wide = jnp.concatenate([west_t, state, east_t], axis=-1)
    wh, wu, wv = wide[0], wide[1], wide[2]

    def widen(row, corners):
        return jnp.concatenate([corners[2][:, None], row, corners[3][:, None]], axis=1)

    def mend(row, corners):
        return jnp.concatenate([
            (row[:, 0] + a * corners[0])[:, None], row[:, 1:-1],
            (row[:, -1] - a * corners[1])[:, None]], axis=1)

    south_v, north_v = widen(south[1], south_corner), widen(north[1], north_corner)
    v_above = jnp.stack([wv[:, 1, 1:-1], north_v], axis=1)
    v_below = jnp.stack([south_v, wv[:, 0, 1:-1]], axis=1)
    h_above = jnp.stack([h[:, 1], north[0]], axis=1)
    h_below = jnp.stack([south[0], h[:, 0]], axis=1)
    spin = f[1:3, None]
    rate_h = -a * ((wu[..., 2:] - wu[..., :-2]) + (v_above - v_below))
    rate_u = -a * (wh[..., 2:] - wh[..., :-2]) + spin * wv[..., 1:-1]
    rate_v = -a * (h_above - h_below) - spin * u
    mid_h = wh[..., 1:-1] + rate_h
    mid_u = wu[..., 1:-1] + rate_u
    mid_v = v + rate_v
    south_mid_h = has_south * (mend(south[2], south_corner) - a * v[:, 0])
    south_mid_v = has_south * (south[3] - a * h[:, 0])
    north_mid_h = has_north * (mend(north[2], north_corner) + a * v[:, 1])
    north_mid_v = has_north * (north[3] + a * h[:, 1])
    mid_v_above = jnp.stack([mid_v[:, 1], north_mid_v], axis=1)
    mid_v_below = jnp.stack([south_mid_v, mid_v[:, 0]], axis=1)
    mid_h_above = jnp.stack([mid_h[:, 1, 1:-1], north_mid_h], axis=1)
    mid_h_below = jnp.stack([south_mid_h, mid_h[:, 0, 1:-1]], axis=1)
    second_h = -a * ((mid_u[..., 2:] - mid_u[..., :-2]) + (mid_v_above - mid_v_below))
    second_u = -a * (mid_h[..., 2:] - mid_h[..., :-2]) + spin * mid_v
    second_v = -a * (mid_h_above - mid_h_below) - spin * mid_u[..., 1:-1]
    forecast = jnp.stack([
        h + 0.5 * (rate_h[..., 1:-1] + second_h),
        u + 0.5 * (rate_u[..., 1:-1] + second_u),
        v + 0.5 * (rate_v + second_v),
    ])

    center = jnp.mean(forecast, axis=1, keepdims=True)
    anomaly = forecast - center

    index = obs_index.reshape(-1)
    slots = index.shape[0]
    entries = 3 * rows * cols
    live = (jnp.arange(slots, dtype=jnp.int32) < obs_count.reshape(())).astype(jnp.float32)
    weight = live / obs_error.reshape(-1)
    weight = weight * weight
    named = (index[:, None] == jnp.arange(entries, dtype=jnp.int32)[None, :]).astype(jnp.float32)
    summed = jnp.dot(
        jnp.stack([weight, weight * observed.reshape(-1)]), named, precision=lax.Precision.HIGHEST
    ).reshape(2, 3, 1, rows, cols)
    weighted = anomaly * summed[0]
    pull = summed[1] - summed[0] * center
    gram = jnp.einsum("fmrc,fnrc->mn", weighted, anomaly, precision=lax.Precision.HIGHEST)
    push = jnp.einsum("frc,fnrc->n", pull[:, 0], anomaly, precision=lax.Precision.HIGHEST)

    row_at = jnp.arange(members)[:, None]
    col_at = jnp.arange(members)[None, :]
    sent = jnp.where((row_at == 0) & (col_at > 0), push[None, :], gram)
    sent = jnp.where((row_at == 1) & (col_at == 2), push[0], sent)
    total = all_sum(sent)
    push = jnp.where(jnp.arange(members) == 0, total[1, 2], total[0])
    lower = jnp.where(row_at >= col_at, total, 0.0)
    gram = lower + jnp.where(row_at > col_at, total, 0.0).T

    identity = jnp.eye(members, dtype=jnp.float32)
    prior = float(members - 1)
    factor = lax.linalg.cholesky(prior * identity + gram, symmetrize_input=False)
    inverse = lax.linalg.triangular_solve(factor, identity, left_side=True, lower=True)
    forward = jnp.dot(inverse, push, precision=lax.Precision.HIGHEST)
    mean_weights = jnp.dot(forward, inverse, precision=lax.Precision.HIGHEST)
    weights = math.sqrt(prior) * inverse + mean_weights[None, :]
    return center + jnp.einsum(
        "fmrc,jm->fjrc", anomaly, weights, precision=lax.Precision.HIGHEST
    )


def solution(mesh):
    lat, lon = mesh.shape["lat"], mesh.shape["lon"]
    parts = Mesh(mesh.devices.reshape(lat // 4, 2, 2, lon // 4, 4), LAT + LON)
    placed = (
        P(None, None, LAT, LON),
        P(LAT, LON, None),
        P(LAT, LON, None),
        P(LAT, LON, None),
        P(LAT, LON),
    )
    return jax.shard_map(
        shards, mesh=parts, in_specs=placed, out_specs=P(None, None, LAT, LON), check_vma=False
    )
```

```python
import math

import jax
import jax.numpy as jnp
from jax import lax
from jax.experimental import pallas as pl
from jax.experimental.pallas import tpu as pltpu
from jax.sharding import Mesh, PartitionSpec as P

HALF_COURANT = 0.4
ROTATION = 0.8
BAND = math.pi / 6.0
LAT = ("x", "zh", "core")
LON = ("zl", "y")
PLANE = ("x", "core", "y")
LINE = ("zh", "zl")
MEMBERS = 128
PANEL = 8


def rotation_at(rows, total_rows):
    latitude = BAND * (2.0 * (rows.astype(jnp.float32) + 0.5) / total_rows - 1.0)
    return ROTATION * jnp.sin(latitude)


def pair_perms(count, periodic):
    inner = [(i, i ^ 1) for i in range(count)]
    outer = []
    for i in range(1, count, 2):
        if i + 1 < count or periodic:
            j = (i + 1) % count
            outer += [(i, j), (j, i)]
    return inner, outer


def swap(low, high, index, axis, perms):
    even = lax.rem(index, 2) == 0
    inner_perm, outer_perm = perms
    outer = lax.ppermute(jnp.where(even, low, high), axis, outer_perm)
    inner = lax.ppermute(jnp.where(even, high, low), axis, inner_perm)
    return jnp.where(even, outer, inner), jnp.where(even, inner, outer)


def all_sum(block):
    plane = lax.axis_size(PLANE)
    line = lax.axis_size(LINE)
    rows, cols = block.shape
    part = rows // plane
    mine = lax.all_to_all(block.reshape(plane, part, cols), PLANE, 0, 0, tiled=True).sum(0)
    mine = lax.all_to_all(
        jnp.broadcast_to(mine[None], (line, part, cols)), LINE, 0, 0, tiled=True
    ).sum(0)
    whole = lax.all_to_all(
        jnp.broadcast_to(mine[None], (plane, part, cols)), PLANE, 0, 0, tiled=True
    )
    return whole.reshape(rows, cols)


def splat(tile, lane):
    return jnp.broadcast_to(tile[:, lane:lane + 1], tile.shape)

def thirds(x):
    hi = x.astype(jnp.bfloat16).astype(jnp.float32)
    rest = x - hi
    mid = rest.astype(jnp.bfloat16).astype(jnp.float32)
    return hi, mid, rest - mid

def outer_sum(left, whole):
    a, b, c = thirds(left)
    d, e, f = thirds(whole)
    first = jnp.concatenate([a, a, b, a, c, b], axis=0).astype(jnp.bfloat16)
    second = jnp.concatenate([d, e, d, f, d, e], axis=0).astype(jnp.bfloat16)
    return lax.dot_general(first, second, (((0,), (0,)), ((), ())), preferred_element_type=jnp.float32)

def eliminate(aug):
    sub = lax.broadcasted_iota(jnp.int32, (PANEL, MEMBERS), 0)
    def fetch(i):
        return (jnp.broadcast_to(aug[i:i+1, :MEMBERS], (PANEL, MEMBERS)), jnp.broadcast_to(aug[i:i+1, MEMBERS:], (PANEL, MEMBERS)))
    left, right = zip(*[fetch(i) for i in range(PANEL)])
    left, right = list(left), list(right)
    s = {(i, k): splat(left[i], k) for i in range(PANEL) for k in range(i, PANEL)}
    for p in range(MEMBERS // PANEL):
        for j in range(PANEL):
            r = lax.rsqrt(s[j, j])
            left[j] = left[j] * r
            right[j] = right[j] * r
            l = {i: s[j, i] * r for i in range(j + 1, PANEL)}
            for i in range(j + 1, PANEL):
                for k in range(i, PANEL):
                    s[i, k] = s[i, k] - l[i] * l[k]
                left[i] = left[i] - l[i] * left[j]
                right[i] = right[i] - l[i] * right[j]
        tl, tr = left[0], right[0]
        for j in range(1, PANEL):
            tl = jnp.where(sub == j, left[j], tl)
            tr = jnp.where(sub == j, right[j], tr)
        aug[p*PANEL:(p+1)*PANEL, MEMBERS:] = tr
        q = p + 1
        if q * PANEL < MEMBERS:
            base = q * PANEL
            t = {(j, i): splat(left[j], base + i) for j in range(PANEL) for i in range(PANEL)}
            nl, nr, ns = [], [], {}
            for i in range(PANEL):
                a, b = fetch(base + i)
                for k in range(i, PANEL):
                    acc = splat(a, base + k)
                    for j in range(PANEL):
                        acc = acc - t[j, i] * t[j, k]
                    ns[i, k] = acc
                for j in range(PANEL):
                    a = a - t[j, i] * left[j]
                    b = b - t[j, i] * right[j]
                nl.append(a); nr.append(b)
            if base + PANEL < MEMBERS:
                prod = outer_sum(tl, jnp.concatenate([tl, tr], axis=1))
                aug[base + PANEL:, :] = aug[base + PANEL:, :] - prod[base + PANEL:, :]
            left, right, s = nl, nr, ns

def finish(total_ref, x_ref, c_ref, o_ref, aug):
    total = total_ref[...]
    row = lax.broadcasted_iota(jnp.int32, (MEMBERS, MEMBERS), 0)
    col = lax.broadcasted_iota(jnp.int32, (MEMBERS, MEMBERS), 1)
    prior = float(MEMBERS - 1)
    unit = jnp.where(row == col, 1.0, 0.0)
    aug[:, :MEMBERS] = jnp.where(col >= row, total, 0.0) + prior * unit
    aug[:, MEMBERS:] = unit
    eliminate(aug)
    inverse = aug[:, MEMBERS:]
    lane = lax.broadcasted_iota(jnp.int32, (8, MEMBERS), 1)
    push = jnp.where(lane == MEMBERS - 1, jnp.broadcast_to(total[MEMBERS-2:MEMBERS-1, 0:1], (8, MEMBERS)), jnp.broadcast_to(total[MEMBERS-1:MEMBERS, :], (8, MEMBERS)))
    forward = lax.dot_general(push, inverse, (((1,), (1,)), ((), ())), precision=lax.Precision.HIGHEST, preferred_element_type=jnp.float32)
    mean_weights = jnp.dot(forward, inverse, precision=lax.Precision.HIGHEST, preferred_element_type=jnp.float32)
    weights = math.sqrt(prior) * inverse + mean_weights[0:1, :]
    for f in range(3):
        for r in range(2):
            k = 2 * f + r
            post = lax.dot_general(weights, x_ref[k * MEMBERS:(k + 1) * MEMBERS, :], (((1,), (1,)), ((), ())), precision=lax.Precision.HIGHEST, preferred_element_type=jnp.float32)
            o_ref[pl.ds(f * 2 * MEMBERS + r, MEMBERS, stride=2), :] = post + c_ref[k:k+1, :]


def shards(prior_ensemble, observed, obs_error, obs_index, obs_count):
    a = HALF_COURANT
    state = prior_ensemble.astype(jnp.float32)
    members, rows, cols = state.shape[1:]
    lat_index, lon_index = lax.axis_index(LAT), lax.axis_index(LON)
    lat_count, lon_count = lax.axis_size(LAT), lax.axis_size(LON)
    lat_perms = pair_perms(lat_count, False)
    lon_perms = pair_perms(lon_count, True)
    total_rows = rows * lat_count
    f = rotation_at(lat_index * rows - 1 + jnp.arange(4, dtype=jnp.int32), total_rows)
    has_south = (lat_index > 0).astype(jnp.float32)
    has_north = (lat_index < lat_count - 1).astype(jnp.float32)

    h, u, v = state[0], state[1], state[2]
    zero = jnp.zeros((members, 1), jnp.float32)

    def slope(row):
        row = jnp.concatenate([zero, row, zero], axis=1)
        return row[:, 2:] - row[:, :-2]

    down = jnp.stack([
        h[:, 0], v[:, 0],
        h[:, 0] - a * slope(u[:, 0]) - a * v[:, 1],
        v[:, 0] - a * h[:, 1] - f[1] * u[:, 0],
    ])
    up = jnp.stack([
        h[:, 1], v[:, 1],
        h[:, 1] - a * slope(u[:, 1]) + a * v[:, 0],
        v[:, 1] + a * h[:, 0] - f[2] * u[:, 1],
    ])
    down, up, edge = lax.optimization_barrier((down, up, state))
    south, north = swap(down, up, lat_index, LAT, lat_perms)

    edge = jnp.transpose(edge, (0, 2, 3, 1))
    west, east = swap(edge[:, :, :2], edge[:, :, -2:], lon_index, LON, lon_perms)

    def corner(row):
        return jnp.stack([west[1, row, 1], east[1, row, 0], west[2, row, 1], east[2, row, 0]])

    south_corner, north_corner = swap(corner(0), corner(1), lat_index, LAT, lat_perms)

    west_t = jnp.transpose(west, (0, 3, 1, 2))
    east_t = jnp.transpose(east, (0, 3, 1, 2))
    wide = jnp.concatenate([west_t, state, east_t], axis=-1)
    wh, wu, wv = wide[0], wide[1], wide[2]

    def widen(row, corners):
        return jnp.concatenate([corners[2][:, None], row, corners[3][:, None]], axis=1)

    def mend(row, corners):
        return jnp.concatenate([
            (row[:, 0] + a * corners[0])[:, None], row[:, 1:-1],
            (row[:, -1] - a * corners[1])[:, None]], axis=1)

    south_v, north_v = widen(south[1], south_corner), widen(north[1], north_corner)
    v_above = jnp.stack([wv[:, 1, 1:-1], north_v], axis=1)
    v_below = jnp.stack([south_v, wv[:, 0, 1:-1]], axis=1)
    h_above = jnp.stack([h[:, 1], north[0]], axis=1)
    h_below = jnp.stack([south[0], h[:, 0]], axis=1)
    spin = f[1:3, None]
    rate_h = -a * ((wu[..., 2:] - wu[..., :-2]) + (v_above - v_below))
    rate_u = -a * (wh[..., 2:] - wh[..., :-2]) + spin * wv[..., 1:-1]
    rate_v = -a * (h_above - h_below) - spin * u
    mid_h = wh[..., 1:-1] + rate_h
    mid_u = wu[..., 1:-1] + rate_u
    mid_v = v + rate_v
    south_mid_h = has_south * (mend(south[2], south_corner) - a * v[:, 0])
    south_mid_v = has_south * (south[3] - a * h[:, 0])
    north_mid_h = has_north * (mend(north[2], north_corner) + a * v[:, 1])
    north_mid_v = has_north * (north[3] + a * h[:, 1])
    mid_v_above = jnp.stack([mid_v[:, 1], north_mid_v], axis=1)
    mid_v_below = jnp.stack([south_mid_v, mid_v[:, 0]], axis=1)
    mid_h_above = jnp.stack([mid_h[:, 1, 1:-1], north_mid_h], axis=1)
    mid_h_below = jnp.stack([south_mid_h, mid_h[:, 0, 1:-1]], axis=1)
    second_h = -a * ((mid_u[..., 2:] - mid_u[..., :-2]) + (mid_v_above - mid_v_below))
    second_u = -a * (mid_h[..., 2:] - mid_h[..., :-2]) + spin * mid_v
    second_v = -a * (mid_h_above - mid_h_below) - spin * mid_u[..., 1:-1]
    forecast = jnp.stack([
        h + 0.5 * (rate_h[..., 1:-1] + second_h),
        u + 0.5 * (rate_u[..., 1:-1] + second_u),
        v + 0.5 * (rate_v + second_v),
    ])

    center = jnp.mean(forecast, axis=1, keepdims=True)
    anomaly = forecast - center

    index = obs_index.reshape(-1)
    slots = index.shape[0]
    entries = 3 * rows * cols
    live = (jnp.arange(slots, dtype=jnp.int32) < obs_count.reshape(())).astype(jnp.float32)
    weight = live / obs_error.reshape(-1)
    weight = weight * weight
    named = (index[:, None] == jnp.arange(entries, dtype=jnp.int32)[None, :]).astype(jnp.float32)
    summed = jnp.dot(
        jnp.stack([weight, weight * observed.reshape(-1)]), named, precision=lax.Precision.HIGHEST
    ).reshape(2, 3, 1, rows, cols)
    weighted = anomaly * summed[0]
    pull = summed[1] - summed[0] * center
    gram = jnp.einsum("fmrc,fnrc->mn", weighted, anomaly, precision=lax.Precision.HIGHEST)
    push = jnp.einsum("frc,fnrc->n", pull[:, 0], anomaly, precision=lax.Precision.HIGHEST)

    row_at = jnp.arange(members)[:, None]
    col_at = jnp.arange(members)[None, :]
    sent = jnp.where((row_at == members - 1) & (col_at < members - 1), push[None, :], gram)
    sent = jnp.where((row_at == members - 2) & (col_at == 0), push[members - 1], sent)
    total = all_sum(sent)
    entries_first = jnp.transpose(anomaly, (0, 2, 3, 1)).reshape(entries, members)
    posterior = pl.pallas_call(
        finish,
        out_shape=jax.ShapeDtypeStruct((3 * rows * members, cols), jnp.float32),
        scratch_shapes=[pltpu.VMEM((members, 2 * members), jnp.float32)],
        compiler_params=pltpu.CompilerParams(vmem_limit_bytes=16 * 1024 * 1024),
        cost_estimate=pl.CostEstimate(flops=3 * 10**7, bytes_accessed=10**6, transcendentals=0),
    )(total, entries_first, center.reshape(3 * rows, cols))
    return posterior.reshape(3, members, rows, cols)


def solution(mesh):
    lat, lon = mesh.shape["lat"], mesh.shape["lon"]
    parts = Mesh(mesh.devices.reshape(lat // 4, 2, 2, lon // 4, 4), LAT + LON)
    placed = (
        P(None, None, LAT, LON),
        P(LAT, LON, None),
        P(LAT, LON, None),
        P(LAT, LON, None),
        P(LAT, LON),
    )
    return jax.shard_map(
        shards, mesh=parts, in_specs=placed, out_specs=P(None, None, LAT, LON), check_vma=False
    )
```

```python
import math

import jax
import jax.numpy as jnp
from jax import lax
from jax.experimental import pallas as pl
from jax.experimental.pallas import tpu as pltpu
from jax.sharding import Mesh, PartitionSpec as P

HALF_COURANT = 0.4
ROTATION = 0.8
BAND = math.pi / 6.0
LAT = ("x", "zh", "core")
LON = ("zl", "y")
PLANE = ("x", "core", "y")
LINE = ("zh", "zl")
MEMBERS = 128
PANEL = 8


def rotation_at(rows, total_rows):
    latitude = BAND * (2.0 * (rows.astype(jnp.float32) + 0.5) / total_rows - 1.0)
    return ROTATION * jnp.sin(latitude)


def pair_perms(count, periodic):
    inner = [(i, i ^ 1) for i in range(count)]
    outer = []
    for i in range(1, count, 2):
        if i + 1 < count or periodic:
            j = (i + 1) % count
            outer += [(i, j), (j, i)]
    return inner, outer


def swap(low, high, even, axis, perms):
    inner_perm, outer_perm = perms
    outer = lax.ppermute(jnp.where(even, low, high), axis, outer_perm)
    inner = lax.ppermute(jnp.where(even, high, low), axis, inner_perm)
    return jnp.where(even, outer, inner), jnp.where(even, inner, outer)


def all_sum(block):
    plane = lax.axis_size(PLANE)
    line = lax.axis_size(LINE)
    rows, cols = block.shape
    part = rows // plane
    mine = lax.all_to_all(block.reshape(plane, part, cols), PLANE, 0, 0, tiled=True).sum(0)
    mine = lax.all_to_all(
        jnp.broadcast_to(mine[None], (line, part, cols)), LINE, 0, 0, tiled=True
    ).sum(0)
    whole = lax.all_to_all(
        jnp.broadcast_to(mine[None], (plane, part, cols)), PLANE, 0, 0, tiled=True
    )
    return whole.reshape(rows, cols)


def splat(tile, lane):
    return jnp.broadcast_to(tile[:, lane:lane + 1], tile.shape)

def thirds(x):
    hi = x.astype(jnp.bfloat16).astype(jnp.float32)
    rest = x - hi
    mid = rest.astype(jnp.bfloat16).astype(jnp.float32)
    return hi, mid, rest - mid

def outer_sum(left, whole):
    a, b, c = thirds(left)
    d, e, f = thirds(whole)
    first = jnp.concatenate([a, a, b, a, c, b], axis=0).astype(jnp.bfloat16)
    second = jnp.concatenate([d, e, d, f, d, e], axis=0).astype(jnp.bfloat16)
    return lax.dot_general(first, second, (((0,), (0,)), ((), ())), preferred_element_type=jnp.float32)

def eliminate(aug):
    sub = lax.broadcasted_iota(jnp.int32, (PANEL, MEMBERS), 0)
    def fetch(i):
        return (jnp.broadcast_to(aug[i:i+1, :MEMBERS], (PANEL, MEMBERS)), jnp.broadcast_to(aug[i:i+1, MEMBERS:], (PANEL, MEMBERS)))
    left, right = zip(*[fetch(i) for i in range(PANEL)])
    left, right = list(left), list(right)
    s = {(i, k): splat(left[i], k) for i in range(PANEL) for k in range(i, PANEL)}
    for p in range(MEMBERS // PANEL):
        for j in range(PANEL):
            r = lax.rsqrt(s[j, j])
            left[j] = left[j] * r
            right[j] = right[j] * r
            l = {i: s[j, i] * r for i in range(j + 1, PANEL)}
            for i in range(j + 1, PANEL):
                for k in range(i, PANEL):
                    s[i, k] = s[i, k] - l[i] * l[k]
                left[i] = left[i] - l[i] * left[j]
                right[i] = right[i] - l[i] * right[j]
        tl, tr = left[0], right[0]
        for j in range(1, PANEL):
            tl = jnp.where(sub == j, left[j], tl)
            tr = jnp.where(sub == j, right[j], tr)
        aug[p*PANEL:(p+1)*PANEL, MEMBERS:] = tr
        q = p + 1
        if q * PANEL < MEMBERS:
            base = q * PANEL
            t = {(j, i): splat(left[j], base + i) for j in range(PANEL) for i in range(PANEL)}
            nl, nr, ns = [], [], {}
            for i in range(PANEL):
                a, b = fetch(base + i)
                for k in range(i, PANEL):
                    acc = splat(a, base + k)
                    for j in range(PANEL):
                        acc = acc - t[j, i] * t[j, k]
                    ns[i, k] = acc
                for j in range(PANEL):
                    a = a - t[j, i] * left[j]
                    b = b - t[j, i] * right[j]
                nl.append(a); nr.append(b)
            if base + PANEL < MEMBERS:
                prod = outer_sum(tl, jnp.concatenate([tl, tr], axis=1))
                aug[base + PANEL:, :] = aug[base + PANEL:, :] - prod[base + PANEL:, :]
            left, right, s = nl, nr, ns

def finish(total_ref, x_ref, c_ref, o_ref, aug):
    total = total_ref[...]
    row = lax.broadcasted_iota(jnp.int32, (MEMBERS, MEMBERS), 0)
    col = lax.broadcasted_iota(jnp.int32, (MEMBERS, MEMBERS), 1)
    prior = float(MEMBERS - 1)
    unit = jnp.where(row == col, 1.0, 0.0)
    aug[:, :MEMBERS] = jnp.where(col >= row, total, 0.0) + prior * unit
    aug[:, MEMBERS:] = unit
    eliminate(aug)
    inverse = aug[:, MEMBERS:]
    lane = lax.broadcasted_iota(jnp.int32, (8, MEMBERS), 1)
    push = jnp.where(lane == MEMBERS - 1, jnp.broadcast_to(total[MEMBERS-2:MEMBERS-1, 0:1], (8, MEMBERS)), jnp.broadcast_to(total[MEMBERS-1:MEMBERS, :], (8, MEMBERS)))
    forward = lax.dot_general(push, inverse, (((1,), (1,)), ((), ())), precision=lax.Precision.HIGHEST, preferred_element_type=jnp.float32)
    mean_weights = jnp.dot(forward, inverse, precision=lax.Precision.HIGHEST, preferred_element_type=jnp.float32)
    weights = math.sqrt(prior) * inverse + mean_weights[0:1, :]
    for f in range(3):
        for r in range(2):
            k = 2 * f + r
            post = lax.dot_general(weights, x_ref[k * MEMBERS:(k + 1) * MEMBERS, :], (((1,), (1,)), ((), ())), precision=lax.Precision.HIGHEST, preferred_element_type=jnp.float32)
            o_ref[pl.ds(f * 2 * MEMBERS + r, MEMBERS, stride=2), :] = post + c_ref[k:k+1, :]


def assimilate(turn_ref, state_ref, west_ref, east_ref, south_ref, north_ref, weight_ref, sent_ref, anomaly_ref, center_ref, wide):
    a = HALF_COURANT
    cols = MEMBERS

    def field(f, r):
        k = 2 * f + r
        return state_ref[k * cols:(k + 1) * cols, :]

    def beside(ref, f, r, c):
        k = (2 * f + r) * 2 + c
        return ref[k:k + 1, :]

    def place(slot, block, low, high):
        wide[slot, 8:8 + cols, :] = block
        wide[slot, 7:8, :] = low
        wide[slot, 8 + cols:9 + cols, :] = high

    def slope(slot):
        return wide[slot, 9:9 + cols, :] - wide[slot, 7:7 + cols, :]

    spin = [turn_ref[1], turn_ref[2]]
    h = [field(0, 0), field(0, 1)]
    u = [field(1, 0), field(1, 1)]
    v = [field(2, 0), field(2, 1)]
    for r in range(2):
        place(4 + r, h[r], beside(west_ref, 0, r, 1), beside(east_ref, 0, r, 0))
        place(6 + r, u[r], beside(west_ref, 1, r, 1), beside(east_ref, 1, r, 0))
    south_h, south_v, south_mid_v, south_mid_h = (south_ref[k * cols:(k + 1) * cols, :] for k in range(4))
    north_h, north_v, north_mid_v, north_mid_h = (north_ref[k * cols:(k + 1) * cols, :] for k in range(4))
    south_edge = [south_ref[4 * cols + k:4 * cols + k + 1, :] for k in range(2)]
    north_edge = [north_ref[4 * cols + k:4 * cols + k + 1, :] for k in range(2)]
    h_below, h_above = [south_h, h[0]], [h[1], north_h]
    v_below, v_above = [south_v, v[0]], [v[1], north_v]
    rate_h, rate_u, rate_v, mid_h, mid_u, mid_v = [], [], [], [], [], []
    for r in range(2):
        rate_h.append(-a * (slope(6 + r) + (v_above[r] - v_below[r])))
        rate_u.append(-a * slope(4 + r) + spin[r] * v[r])
        rate_v.append(-a * (h_above[r] - h_below[r]) - spin[r] * u[r])
        mid_h.append(h[r] + rate_h[r])
        mid_u.append(u[r] + rate_u[r])
        mid_v.append(v[r] + rate_v[r])
    for r in range(2):
        outside_h, outside_u = [], []
        for side, ref in enumerate((west_ref, east_ref)):
            near, far = (1, 0) if side == 0 else (0, 1)
            inner_h = h[r][0:1, :] if side == 0 else h[r][cols - 1:cols, :]
            inner_u = u[r][0:1, :] if side == 0 else u[r][cols - 1:cols, :]
            sign = -a if side == 0 else a
            own = [beside(ref, 2, 0, near), beside(ref, 2, 1, near)]
            below = south_edge[side] if r == 0 else own[0]
            above = own[1] if r == 0 else north_edge[side]
            outside_h.append(
                beside(ref, 0, r, near) + sign * (inner_u - beside(ref, 1, r, far)) - a * (above - below)
            )
            outside_u.append(
                beside(ref, 1, r, near) + sign * (inner_h - beside(ref, 0, r, far)) + spin[r] * own[r]
            )
        place(r, mid_h[r], *outside_h)
        place(2 + r, mid_u[r], *outside_u)
    has_south, has_north = turn_ref[4], turn_ref[5]
    south_mid_h = has_south * (south_mid_h - a * v[0])
    south_mid_v = has_south * (south_mid_v - a * h[0])
    north_mid_h = has_north * (north_mid_h + a * v[1])
    north_mid_v = has_north * (north_mid_v + a * h[1])
    mid_h_below, mid_h_above = [south_mid_h, mid_h[0]], [mid_h[1], north_mid_h]
    mid_v_below, mid_v_above = [south_mid_v, mid_v[0]], [mid_v[1], north_mid_v]
    forecast = [None] * 6
    for r in range(2):
        second_h = -a * (slope(2 + r) + (mid_v_above[r] - mid_v_below[r]))
        second_u = -a * slope(r) + spin[r] * mid_v[r]
        second_v = -a * (mid_h_above[r] - mid_h_below[r]) - spin[r] * mid_u[r]
        forecast[r] = h[r] + 0.5 * (rate_h[r] + second_h)
        forecast[2 + r] = u[r] + 0.5 * (rate_u[r] + second_u)
        forecast[4 + r] = v[r] + 0.5 * (rate_v[r] + second_v)
    share = jnp.full((8, MEMBERS), 1.0 / MEMBERS, jnp.float32)
    push = jnp.zeros((1, MEMBERS), jnp.float32)
    gram = jnp.zeros((MEMBERS, MEMBERS), jnp.float32)
    for k in range(6):
        mean = jnp.sum(forecast[k], axis=1, keepdims=True) * (1.0 / MEMBERS)
        anomaly = forecast[k] - mean
        anomaly_ref[k * cols:(k + 1) * cols, :] = anomaly
        row = lax.dot_general(
            share, forecast[k], (((1,), (1,)), ((), ())), precision=lax.Precision.HIGHEST,
            preferred_element_type=jnp.float32,
        )
        center_ref[k:k + 1, :] = row[0:1, :]
        weight = weight_ref[k * cols:(k + 1) * cols, 0:1]
        pull = weight_ref[k * cols:(k + 1) * cols, 1:2] - weight * mean
        push = push + jnp.sum(pull * anomaly, axis=0, keepdims=True)
        gram = gram + lax.dot_general(
            weight * anomaly, anomaly, (((0,), (0,)), ((), ())), precision=lax.Precision.HIGHEST,
            preferred_element_type=jnp.float32,
        )
    row_at = lax.broadcasted_iota(jnp.int32, (MEMBERS, MEMBERS), 0)
    col_at = lax.broadcasted_iota(jnp.int32, (MEMBERS, MEMBERS), 1)
    sent = jnp.where((row_at == MEMBERS - 1) & (col_at < MEMBERS - 1), push, gram)
    sent_ref[...] = jnp.where((row_at == MEMBERS - 2) & (col_at == 0), push[:, MEMBERS - 1:], sent)


def shards(prior_ensemble, observed, obs_error, obs_index, obs_count):
    a = HALF_COURANT
    members, rows, cols = prior_ensemble.shape[1:]
    entries = 3 * rows * cols
    lat_index, lon_index = lax.axis_index(LAT), lax.axis_index(LON)
    lat_count, lon_count = lax.axis_size(LAT), lax.axis_size(LON)
    lat_perms = pair_perms(lat_count, False)
    lon_perms = pair_perms(lon_count, True)
    lat_even, lon_even = lax.rem(lat_index, 2) == 0, lax.rem(lon_index, 2) == 0
    total_rows = rows * lat_count
    turn = rotation_at(lat_index * rows - 1 + jnp.arange(4, dtype=jnp.int32), total_rows)
    has_south = (lat_index > 0).astype(jnp.float32)
    has_north = (lat_index < lat_count - 1).astype(jnp.float32)

    state = jnp.transpose(prior_ensemble, (0, 2, 3, 1)).astype(jnp.float32)
    west, east = swap(state[:, :, :2], state[:, :, -2:], lon_even, LON, lon_perms)

    inner_perm, outer_perm = lat_perms
    h, u, v = state[0], state[1], state[2]

    def early(row, other, sign, spin):
        return jnp.concatenate([h[row], v[row], v[row] + sign * a * h[other] - spin * u[row]])

    down_early, up_early = early(0, 1, -1.0, turn[1]), early(1, 0, 1.0, turn[2])
    outer_early = lax.ppermute(jnp.where(lat_even, down_early, up_early), LAT, outer_perm)

    def late(row, other, sign):
        around = jnp.concatenate([west[1, row, 1:], u[row], east[1, row, :1]])
        mid = h[row] - a * (around[2:] - around[:-2]) + sign * a * v[other]
        return jnp.concatenate([mid, west[2, row, 1:], east[2, row, :1]])

    down_late, up_late = late(0, 1, -1.0), late(1, 0, 1.0)
    outer_late = lax.ppermute(jnp.where(lat_even, down_late, up_late), LAT, outer_perm)
    inner = lax.ppermute(
        jnp.where(
            lat_even, jnp.concatenate([up_early, up_late]), jnp.concatenate([down_early, down_late])
        ),
        LAT, inner_perm,
    )
    outer = jnp.concatenate([outer_early, outer_late])
    south, north = jnp.where(lat_even, outer, inner), jnp.where(lat_even, inner, outer)

    index = obs_index.reshape(-1)
    slots = index.shape[0]
    live = (jnp.arange(slots, dtype=jnp.int32) < obs_count.reshape(())).astype(jnp.float32)
    weight = live / obs_error.reshape(-1)
    weight = weight * weight
    named = (jnp.arange(entries, dtype=jnp.int32)[:, None] == index[None, :]).astype(jnp.float32)
    weights = jnp.dot(
        named, jnp.stack([weight, weight * observed.reshape(-1)], axis=1), precision=lax.Precision.HIGHEST
    )
    scalars = jnp.concatenate([turn, jnp.stack([has_south, has_north])])
    vmem = pl.BlockSpec(memory_space=pltpu.VMEM)
    sent, anomaly, center = pl.pallas_call(
        assimilate,
        in_specs=[pl.BlockSpec(memory_space=pltpu.SMEM)] + [vmem] * 6,
        out_specs=[vmem] * 3,
        out_shape=[
            jax.ShapeDtypeStruct((members, members), jnp.float32),
            jax.ShapeDtypeStruct((entries, members), jnp.float32),
            jax.ShapeDtypeStruct((3 * rows, cols), jnp.float32),
        ],
        scratch_shapes=[pltpu.VMEM((8, cols + 16, members), jnp.float32)],
        compiler_params=pltpu.CompilerParams(vmem_limit_bytes=16 * 1024 * 1024),
        cost_estimate=pl.CostEstimate(flops=3 * 10**7, bytes_accessed=2 * 10**6, transcendentals=0),
    )(
        scalars, state.reshape(entries, members), west.reshape(-1, members), east.reshape(-1, members),
        south, north, weights,
    )
    total = all_sum(sent)
    posterior = pl.pallas_call(
        finish,
        out_shape=jax.ShapeDtypeStruct((entries, cols), jnp.float32),
        scratch_shapes=[pltpu.VMEM((members, 2 * members), jnp.float32)],
        compiler_params=pltpu.CompilerParams(vmem_limit_bytes=16 * 1024 * 1024),
        cost_estimate=pl.CostEstimate(flops=3 * 10**7, bytes_accessed=10**6, transcendentals=0),
    )(total, anomaly, center)
    return posterior.reshape(3, members, rows, cols)


def solution(mesh):
    lat, lon = mesh.shape["lat"], mesh.shape["lon"]
    parts = Mesh(mesh.devices.reshape(lat // 4, 2, 2, lon // 4, 4), LAT + LON)
    placed = (
        P(None, None, LAT, LON),
        P(LAT, LON, None),
        P(LAT, LON, None),
        P(LAT, LON, None),
        P(LAT, LON),
    )
    return jax.shard_map(
        shards, mesh=parts, in_specs=placed, out_specs=P(None, None, LAT, LON), check_vma=False
    )
```

```python
import math

import jax
import jax.numpy as jnp
from jax import lax
from jax.experimental import pallas as pl
from jax.experimental.pallas import tpu as pltpu
from jax.sharding import Mesh, PartitionSpec as P

HALF_COURANT = 0.4
ROTATION = 0.8
BAND = math.pi / 6.0
LAT = ("x", "zh", "core")
LON = ("zl", "y")
PLANE = ("x", "core", "y")
LINE = ("zh", "zl")
MEMBERS = 128
PANEL = 8


def rotation_at(rows, total_rows):
    latitude = BAND * (2.0 * (rows.astype(jnp.float32) + 0.5) / total_rows - 1.0)
    return ROTATION * jnp.sin(latitude)


def pair_perms(count, periodic):
    inner = [(i, i ^ 1) for i in range(count)]
    outer = []
    for i in range(1, count, 2):
        if i + 1 < count or periodic:
            j = (i + 1) % count
            outer += [(i, j), (j, i)]
    return inner, outer


def all_sum(block):
    plane = lax.axis_size(PLANE)
    line = lax.axis_size(LINE)
    rows, cols = block.shape
    part = rows // plane
    mine = lax.all_to_all(block.reshape(plane, part, cols), PLANE, 0, 0, tiled=True).sum(0)
    mine = lax.all_to_all(
        jnp.broadcast_to(mine[None], (line, part, cols)), LINE, 0, 0, tiled=True
    ).sum(0)
    whole = lax.all_to_all(
        jnp.broadcast_to(mine[None], (plane, part, cols)), PLANE, 0, 0, tiled=True
    )
    return whole.reshape(rows, cols)


def splat(tile, lane):
    return jnp.broadcast_to(tile[:, lane:lane + 1], tile.shape)

def thirds(x):
    hi = x.astype(jnp.bfloat16).astype(jnp.float32)
    rest = x - hi
    mid = rest.astype(jnp.bfloat16).astype(jnp.float32)
    return hi, mid, rest - mid

def outer_sum(left, whole):
    a, b, c = thirds(left)
    d, e, f = thirds(whole)
    first = jnp.concatenate([a, a, b, a, c, b], axis=0).astype(jnp.bfloat16)
    second = jnp.concatenate([d, e, d, f, d, e], axis=0).astype(jnp.bfloat16)
    return lax.dot_general(first, second, (((0,), (0,)), ((), ())), preferred_element_type=jnp.float32)

def eliminate(aug):
    sub = lax.broadcasted_iota(jnp.int32, (PANEL, MEMBERS), 0)
    def fetch(i):
        return (jnp.broadcast_to(aug[i:i+1, :MEMBERS], (PANEL, MEMBERS)), jnp.broadcast_to(aug[i:i+1, MEMBERS:], (PANEL, MEMBERS)))
    left, right = zip(*[fetch(i) for i in range(PANEL)])
    left, right = list(left), list(right)
    s = {(i, k): splat(left[i], k) for i in range(PANEL) for k in range(i, PANEL)}
    for p in range(MEMBERS // PANEL):
        for j in range(PANEL):
            r = lax.rsqrt(s[j, j])
            left[j] = left[j] * r
            right[j] = right[j] * r
            l = {i: s[j, i] * r for i in range(j + 1, PANEL)}
            for i in range(j + 1, PANEL):
                for k in range(i, PANEL):
                    s[i, k] = s[i, k] - l[i] * l[k]
                left[i] = left[i] - l[i] * left[j]
                right[i] = right[i] - l[i] * right[j]
        tl, tr = left[0], right[0]
        for j in range(1, PANEL):
            tl = jnp.where(sub == j, left[j], tl)
            tr = jnp.where(sub == j, right[j], tr)
        aug[p*PANEL:(p+1)*PANEL, MEMBERS:] = tr
        q = p + 1
        if q * PANEL < MEMBERS:
            base = q * PANEL
            t = {(j, i): splat(left[j], base + i) for j in range(PANEL) for i in range(PANEL)}
            nl, nr, ns = [], [], {}
            for i in range(PANEL):
                a, b = fetch(base + i)
                for k in range(i, PANEL):
                    acc = splat(a, base + k)
                    for j in range(PANEL):
                        acc = acc - t[j, i] * t[j, k]
                    ns[i, k] = acc
                for j in range(PANEL):
                    a = a - t[j, i] * left[j]
                    b = b - t[j, i] * right[j]
                nl.append(a); nr.append(b)
            if base + PANEL < MEMBERS:
                prod = outer_sum(tl, jnp.concatenate([tl, tr], axis=1))
                aug[base + PANEL:, :] = aug[base + PANEL:, :] - prod[base + PANEL:, :]
            left, right, s = nl, nr, ns

def finish(total_ref, x_ref, c_ref, o_ref, aug):
    total = total_ref[...]
    row = lax.broadcasted_iota(jnp.int32, (MEMBERS, MEMBERS), 0)
    col = lax.broadcasted_iota(jnp.int32, (MEMBERS, MEMBERS), 1)
    prior = float(MEMBERS - 1)
    unit = jnp.where(row == col, 1.0, 0.0)
    aug[:, :MEMBERS] = jnp.where(col >= row, total, 0.0) + prior * unit
    aug[:, MEMBERS:] = unit
    eliminate(aug)
    inverse = aug[:, MEMBERS:]
    lane = lax.broadcasted_iota(jnp.int32, (8, MEMBERS), 1)
    push = jnp.where(lane == MEMBERS - 1, jnp.broadcast_to(total[MEMBERS-2:MEMBERS-1, 0:1], (8, MEMBERS)), jnp.broadcast_to(total[MEMBERS-1:MEMBERS, :], (8, MEMBERS)))
    forward = lax.dot_general(push, inverse, (((1,), (1,)), ((), ())), precision=lax.Precision.HIGHEST, preferred_element_type=jnp.float32)
    mean_weights = jnp.dot(forward, inverse, precision=lax.Precision.HIGHEST, preferred_element_type=jnp.float32)
    weights = math.sqrt(prior) * inverse + mean_weights[0:1, :]
    for f in range(3):
        for r in range(2):
            k = 2 * f + r
            post = lax.dot_general(weights, x_ref[k * MEMBERS:(k + 1) * MEMBERS, :], (((1,), (1,)), ((), ())), precision=lax.Precision.HIGHEST, preferred_element_type=jnp.float32)
            o_ref[pl.ds(f * 2 * MEMBERS + r, MEMBERS, stride=2), :] = post + c_ref[k:k+1, :]


def turned(even_ref, prior_ref, state_ref, outer_ref, inner_ref, rows_ref):
    cols = MEMBERS
    even = even_ref[0] > 0
    for f in range(3):
        rows_ref[...] = prior_ref[2 * cols * f:2 * cols * (f + 1), :].astype(jnp.float32)
        for r in range(2):
            k = 2 * f + r
            block = rows_ref[pl.ds(r, cols, stride=2), :].T
            state_ref[k * cols:(k + 1) * cols, :] = block
            low, high = block[:2, :], block[cols - 2:, :]
            outer_ref[2 * k:2 * k + 2, :] = jnp.where(even, low, high)
            inner_ref[2 * k:2 * k + 2, :] = jnp.where(even, high, low)


def early_rows(turn_ref, state_ref, out_ref):
    row = turn_ref[6].astype(jnp.int32)
    other = 1 - row
    sign = 2.0 * turn_ref[6] - 1.0
    spin = turn_ref[1 + row]
    cols = MEMBERS

    def field(f, r):
        return state_ref[pl.ds(pl.multiple_of((2 * f + r) * cols, cols), cols), :]

    h, v = field(0, row), field(2, row)
    out_ref[:cols, :] = h
    out_ref[cols:2 * cols, :] = v
    out_ref[2 * cols:, :] = v + (sign * HALF_COURANT) * field(0, other) - spin * field(1, row)


def edge_rows(state_ref, west_ref, east_ref, wide, row, sign):
    cols = MEMBERS

    def field(f, r):
        return state_ref[pl.ds(pl.multiple_of((2 * f + r) * cols, cols), cols), :]

    def beside(ref, f, c):
        return ref[pl.ds((2 * f + row) * 2 + c, 1), :]

    wide[8:8 + cols, :] = field(1, row)
    wide[7:8, :] = beside(west_ref, 1, 1)
    wide[8 + cols:9 + cols, :] = beside(east_ref, 1, 0)
    slope = wide[9:9 + cols, :] - wide[7:7 + cols, :]
    mid = field(0, row) - HALF_COURANT * slope + (sign * HALF_COURANT) * field(2, 1 - row)
    return field, mid, beside(west_ref, 2, 1), beside(east_ref, 2, 0)


def late_rows(turn_ref, state_ref, west_ref, east_ref, out_ref, wide):
    cols = MEMBERS
    row = turn_ref[6].astype(jnp.int32)
    _, mid, west_v, east_v = edge_rows(
        state_ref, west_ref, east_ref, wide, row, 2.0 * turn_ref[6] - 1.0
    )
    out_ref[:cols, :] = mid
    out_ref[cols:cols + 1, :] = west_v
    out_ref[cols + 1:cols + 2, :] = east_v


def inner_rows(turn_ref, state_ref, west_ref, east_ref, out_ref, wide):
    cols = MEMBERS
    row = 1 - turn_ref[6].astype(jnp.int32)
    sign = 1.0 - 2.0 * turn_ref[6]
    field, mid, west_v, east_v = edge_rows(state_ref, west_ref, east_ref, wide, row, sign)
    h, v = field(0, row), field(2, row)
    out_ref[:cols, :] = h
    out_ref[cols:2 * cols, :] = v
    out_ref[2 * cols:3 * cols, :] = (
        v + (sign * HALF_COURANT) * field(0, 1 - row) - turn_ref[1 + row] * field(1, row)
    )
    out_ref[3 * cols:4 * cols, :] = mid
    out_ref[4 * cols:4 * cols + 1, :] = west_v
    out_ref[4 * cols + 1:4 * cols + 2, :] = east_v


def assimilate(turn_ref, state_ref, west_ref, east_ref, south_ref, north_ref, weight_ref, sent_ref, anomaly_ref, center_ref, wide):
    a = HALF_COURANT
    cols = MEMBERS

    def field(f, r):
        k = 2 * f + r
        return state_ref[k * cols:(k + 1) * cols, :]

    def beside(ref, f, r, c):
        k = (2 * f + r) * 2 + c
        return ref[k:k + 1, :]

    def place(slot, block, low, high):
        wide[slot, 8:8 + cols, :] = block
        wide[slot, 7:8, :] = low
        wide[slot, 8 + cols:9 + cols, :] = high

    def slope(slot):
        return wide[slot, 9:9 + cols, :] - wide[slot, 7:7 + cols, :]

    spin = [turn_ref[1], turn_ref[2]]
    h = [field(0, 0), field(0, 1)]
    u = [field(1, 0), field(1, 1)]
    v = [field(2, 0), field(2, 1)]
    for r in range(2):
        place(4 + r, h[r], beside(west_ref, 0, r, 1), beside(east_ref, 0, r, 0))
        place(6 + r, u[r], beside(west_ref, 1, r, 1), beside(east_ref, 1, r, 0))
    south_h, south_v, south_mid_v, south_mid_h = (south_ref[k * cols:(k + 1) * cols, :] for k in range(4))
    north_h, north_v, north_mid_v, north_mid_h = (north_ref[k * cols:(k + 1) * cols, :] for k in range(4))
    south_edge = [south_ref[4 * cols + k:4 * cols + k + 1, :] for k in range(2)]
    north_edge = [north_ref[4 * cols + k:4 * cols + k + 1, :] for k in range(2)]
    h_below, h_above = [south_h, h[0]], [h[1], north_h]
    v_below, v_above = [south_v, v[0]], [v[1], north_v]
    rate_h, rate_u, rate_v, mid_h, mid_u, mid_v = [], [], [], [], [], []
    for r in range(2):
        rate_h.append(-a * (slope(6 + r) + (v_above[r] - v_below[r])))
        rate_u.append(-a * slope(4 + r) + spin[r] * v[r])
        rate_v.append(-a * (h_above[r] - h_below[r]) - spin[r] * u[r])
        mid_h.append(h[r] + rate_h[r])
        mid_u.append(u[r] + rate_u[r])
        mid_v.append(v[r] + rate_v[r])
    for r in range(2):
        outside_h, outside_u = [], []
        for side, ref in enumerate((west_ref, east_ref)):
            near, far = (1, 0) if side == 0 else (0, 1)
            inner_h = h[r][0:1, :] if side == 0 else h[r][cols - 1:cols, :]
            inner_u = u[r][0:1, :] if side == 0 else u[r][cols - 1:cols, :]
            sign = -a if side == 0 else a
            own = [beside(ref, 2, 0, near), beside(ref, 2, 1, near)]
            below = south_edge[side] if r == 0 else own[0]
            above = own[1] if r == 0 else north_edge[side]
            outside_h.append(
                beside(ref, 0, r, near) + sign * (inner_u - beside(ref, 1, r, far)) - a * (above - below)
            )
            outside_u.append(
                beside(ref, 1, r, near) + sign * (inner_h - beside(ref, 0, r, far)) + spin[r] * own[r]
            )
        place(r, mid_h[r], *outside_h)
        place(2 + r, mid_u[r], *outside_u)
    has_south, has_north = turn_ref[4], turn_ref[5]
    south_mid_h = has_south * (south_mid_h - a * v[0])
    south_mid_v = has_south * (south_mid_v - a * h[0])
    north_mid_h = has_north * (north_mid_h + a * v[1])
    north_mid_v = has_north * (north_mid_v + a * h[1])
    mid_h_below, mid_h_above = [south_mid_h, mid_h[0]], [mid_h[1], north_mid_h]
    mid_v_below, mid_v_above = [south_mid_v, mid_v[0]], [mid_v[1], north_mid_v]
    forecast = [None] * 6
    for r in range(2):
        second_h = -a * (slope(2 + r) + (mid_v_above[r] - mid_v_below[r]))
        second_u = -a * slope(r) + spin[r] * mid_v[r]
        second_v = -a * (mid_h_above[r] - mid_h_below[r]) - spin[r] * mid_u[r]
        forecast[r] = h[r] + 0.5 * (rate_h[r] + second_h)
        forecast[2 + r] = u[r] + 0.5 * (rate_u[r] + second_u)
        forecast[4 + r] = v[r] + 0.5 * (rate_v[r] + second_v)
    share = jnp.full((8, MEMBERS), 1.0 / MEMBERS, jnp.float32)
    push = jnp.zeros((1, MEMBERS), jnp.float32)
    gram = jnp.zeros((MEMBERS, MEMBERS), jnp.float32)
    for k in range(6):
        mean = jnp.sum(forecast[k], axis=1, keepdims=True) * (1.0 / MEMBERS)
        anomaly = forecast[k] - mean
        anomaly_ref[k * cols:(k + 1) * cols, :] = anomaly
        row = lax.dot_general(
            share, forecast[k], (((1,), (1,)), ((), ())), precision=lax.Precision.HIGHEST,
            preferred_element_type=jnp.float32,
        )
        center_ref[k:k + 1, :] = row[0:1, :]
        weight = weight_ref[k * cols:(k + 1) * cols, 0:1]
        pull = weight_ref[k * cols:(k + 1) * cols, 1:2] - weight * mean
        push = push + jnp.sum(pull * anomaly, axis=0, keepdims=True)
        gram = gram + lax.dot_general(
            weight * anomaly, anomaly, (((0,), (0,)), ((), ())), precision=lax.Precision.HIGHEST,
            preferred_element_type=jnp.float32,
        )
    row_at = lax.broadcasted_iota(jnp.int32, (MEMBERS, MEMBERS), 0)
    col_at = lax.broadcasted_iota(jnp.int32, (MEMBERS, MEMBERS), 1)
    sent = jnp.where((row_at == MEMBERS - 1) & (col_at < MEMBERS - 1), push, gram)
    sent_ref[...] = jnp.where((row_at == MEMBERS - 2) & (col_at == 0), push[:, MEMBERS - 1:], sent)


def shards(prior_ensemble, observed, obs_error, obs_index, obs_count):
    a = HALF_COURANT
    members, rows, cols = prior_ensemble.shape[1:]
    entries = 3 * rows * cols
    lat_index, lon_index = lax.axis_index(LAT), lax.axis_index(LON)
    lat_count, lon_count = lax.axis_size(LAT), lax.axis_size(LON)
    lat_perms = pair_perms(lat_count, False)
    lon_perms = pair_perms(lon_count, True)
    lat_even, lon_even = lax.rem(lat_index, 2) == 0, lax.rem(lon_index, 2) == 0
    total_rows = rows * lat_count
    turn = rotation_at(lat_index * rows - 1 + jnp.arange(4, dtype=jnp.int32), total_rows)
    has_south = (lat_index > 0).astype(jnp.float32)
    has_north = (lat_index < lat_count - 1).astype(jnp.float32)

    smem = pl.BlockSpec(memory_space=pltpu.SMEM)
    vmem = pl.BlockSpec(memory_space=pltpu.VMEM)
    params = pltpu.CompilerParams(vmem_limit_bytes=16 * 1024 * 1024)
    edges = 2 * 3 * rows
    state, outer_edge, inner_edge = pl.pallas_call(
        turned,
        in_specs=[smem, vmem],
        out_specs=[vmem] * 3,
        out_shape=[
            jax.ShapeDtypeStruct((entries, members), jnp.float32),
            jax.ShapeDtypeStruct((edges, members), jnp.float32),
            jax.ShapeDtypeStruct((edges, members), jnp.float32),
        ],
        scratch_shapes=[pltpu.VMEM((rows * members, cols), jnp.float32)],
        compiler_params=params,
        cost_estimate=pl.CostEstimate(flops=10**5, bytes_accessed=6 * 10**5, transcendentals=0),
    )(lon_even.astype(jnp.int32).reshape(1), prior_ensemble.reshape(entries, cols))
    lon_inner, lon_outer = lon_perms
    outer_edge = lax.ppermute(outer_edge, LON, lon_outer)
    inner_edge = lax.ppermute(inner_edge, LON, lon_inner)
    west = jnp.where(lon_even, outer_edge, inner_edge)
    east = jnp.where(lon_even, inner_edge, outer_edge)

    inner_perm, outer_perm = lat_perms
    edge_row = 1.0 - lat_even.astype(jnp.float32)
    scalars = jnp.concatenate([turn, jnp.stack([has_south, has_north, edge_row])])
    outer_early = pl.pallas_call(
        early_rows,
        in_specs=[smem, vmem],
        out_specs=vmem,
        out_shape=jax.ShapeDtypeStruct((3 * cols, members), jnp.float32),
        compiler_params=params,
        cost_estimate=pl.CostEstimate(flops=10**5, bytes_accessed=10**5, transcendentals=0),
    )(scalars, state)
    outer_early = lax.ppermute(outer_early, LAT, outer_perm)

    def edge_call(kernel, height):
        return pl.pallas_call(
            kernel,
            in_specs=[smem] + [vmem] * 3,
            out_specs=vmem,
            out_shape=jax.ShapeDtypeStruct((height, members), jnp.float32),
            scratch_shapes=[pltpu.VMEM((cols + 16, members), jnp.float32)],
            compiler_params=params,
            cost_estimate=pl.CostEstimate(flops=10**5, bytes_accessed=10**5, transcendentals=0),
        )(scalars, state, west, east)

    outer_late = lax.ppermute(edge_call(late_rows, cols + 2), LAT, outer_perm)
    inner = lax.ppermute(edge_call(inner_rows, 4 * cols + 2), LAT, inner_perm)
    outer = jnp.concatenate([outer_early, outer_late])
    south, north = jnp.where(lat_even, outer, inner), jnp.where(lat_even, inner, outer)

    index = obs_index.reshape(-1)
    slots = index.shape[0]
    live = (jnp.arange(slots, dtype=jnp.int32) < obs_count.reshape(())).astype(jnp.float32)
    weight = live / obs_error.reshape(-1)
    weight = weight * weight
    named = (jnp.arange(entries, dtype=jnp.int32)[:, None] == index[None, :]).astype(jnp.float32)
    weights = jnp.dot(
        named, jnp.stack([weight, weight * observed.reshape(-1)], axis=1), precision=lax.Precision.HIGHEST
    )
    sent, anomaly, center = pl.pallas_call(
        assimilate,
        in_specs=[smem] + [vmem] * 6,
        out_specs=[vmem] * 3,
        out_shape=[
            jax.ShapeDtypeStruct((members, members), jnp.float32),
            jax.ShapeDtypeStruct((entries, members), jnp.float32),
            jax.ShapeDtypeStruct((3 * rows, cols), jnp.float32),
        ],
        scratch_shapes=[pltpu.VMEM((8, cols + 16, members), jnp.float32)],
        compiler_params=params,
        cost_estimate=pl.CostEstimate(flops=3 * 10**7, bytes_accessed=2 * 10**6, transcendentals=0),
    )(
        scalars, state, west, east, south, north, weights,
    )
    total = all_sum(sent)
    posterior = pl.pallas_call(
        finish,
        out_shape=jax.ShapeDtypeStruct((entries, cols), jnp.float32),
        scratch_shapes=[pltpu.VMEM((members, 2 * members), jnp.float32)],
        compiler_params=params,
        cost_estimate=pl.CostEstimate(flops=3 * 10**7, bytes_accessed=10**6, transcendentals=0),
    )(total, anomaly, center)
    return posterior.reshape(3, members, rows, cols)


def solution(mesh):
    lat, lon = mesh.shape["lat"], mesh.shape["lon"]
    parts = Mesh(mesh.devices.reshape(lat // 4, 2, 2, lon // 4, 4), LAT + LON)
    placed = (
        P(None, None, LAT, LON),
        P(LAT, LON, None),
        P(LAT, LON, None),
        P(LAT, LON, None),
        P(LAT, LON),
    )
    return jax.shard_map(
        shards, mesh=parts, in_specs=placed, out_specs=P(None, None, LAT, LON), check_vma=False
    )
```

```python
import math

import jax
import jax.numpy as jnp
from jax import lax
from jax.experimental import pallas as pl
from jax.experimental.pallas import tpu as pltpu
from jax.sharding import Mesh, PartitionSpec as P

HALF_COURANT = 0.4
ROTATION = 0.8
BAND = math.pi / 6.0
LAT = ("x", "zh", "core")
LON = ("zl", "y")
PLANE = ("x", "core", "y")
LINE = ("zh", "zl")
MEMBERS = 128
PANEL = 8


def rotation_at(rows, total_rows):
    latitude = BAND * (2.0 * (rows.astype(jnp.float32) + 0.5) / total_rows - 1.0)
    return ROTATION * jnp.sin(latitude)


def pair_perms(count, periodic):
    inner = [(i, i ^ 1) for i in range(count)]
    outer = []
    for i in range(1, count, 2):
        if i + 1 < count or periodic:
            j = (i + 1) % count
            outer += [(i, j), (j, i)]
    return inner, outer


def all_sum(block):
    plane = lax.axis_size(PLANE)
    line = lax.axis_size(LINE)
    rows, cols = block.shape
    part = rows // plane
    mine = lax.all_to_all(block.reshape(plane, part, cols), PLANE, 0, 0, tiled=True).sum(0)
    mine = lax.all_to_all(
        jnp.broadcast_to(mine[None], (line, part, cols)), LINE, 0, 0, tiled=True
    ).sum(0)
    whole = lax.all_to_all(
        jnp.broadcast_to(mine[None], (plane, part, cols)), PLANE, 0, 0, tiled=True
    )
    return whole.reshape(rows, cols)


def splat(tile, lane):
    return jnp.broadcast_to(tile[:, lane:lane + 1], tile.shape)

def thirds(x):
    hi = x.astype(jnp.bfloat16).astype(jnp.float32)
    rest = x - hi
    mid = rest.astype(jnp.bfloat16).astype(jnp.float32)
    return hi, mid, rest - mid

def outer_sum(left, whole):
    a, b, c = thirds(left)
    d, e, f = thirds(whole)
    first = jnp.concatenate([a, a, b, a, c, b], axis=0).astype(jnp.bfloat16)
    second = jnp.concatenate([d, e, d, f, d, e], axis=0).astype(jnp.bfloat16)
    return lax.dot_general(first, second, (((0,), (0,)), ((), ())), preferred_element_type=jnp.float32)

def eliminate(aug):
    sub = lax.broadcasted_iota(jnp.int32, (PANEL, MEMBERS), 0)
    def fetch(i):
        return (jnp.broadcast_to(aug[i:i+1, :MEMBERS], (PANEL, MEMBERS)), jnp.broadcast_to(aug[i:i+1, MEMBERS:], (PANEL, MEMBERS)))
    left, right = zip(*[fetch(i) for i in range(PANEL)])
    left, right = list(left), list(right)
    s = {(i, k): splat(left[i], k) for i in range(PANEL) for k in range(i, PANEL)}
    for p in range(MEMBERS // PANEL):
        for j in range(PANEL):
            r = lax.rsqrt(s[j, j])
            left[j] = left[j] * r
            right[j] = right[j] * r
            l = {i: s[j, i] * r for i in range(j + 1, PANEL)}
            for i in range(j + 1, PANEL):
                for k in range(i, PANEL):
                    s[i, k] = s[i, k] - l[i] * l[k]
                left[i] = left[i] - l[i] * left[j]
                right[i] = right[i] - l[i] * right[j]
        tl, tr = left[0], right[0]
        for j in range(1, PANEL):
            tl = jnp.where(sub == j, left[j], tl)
            tr = jnp.where(sub == j, right[j], tr)
        aug[p*PANEL:(p+1)*PANEL, MEMBERS:] = tr
        q = p + 1
        if q * PANEL < MEMBERS:
            base = q * PANEL
            t = {(j, i): splat(left[j], base + i) for j in range(PANEL) for i in range(PANEL)}
            nl, nr, ns = [], [], {}
            for i in range(PANEL):
                a, b = fetch(base + i)
                for k in range(i, PANEL):
                    acc = splat(a, base + k)
                    for j in range(PANEL):
                        acc = acc - t[j, i] * t[j, k]
                    ns[i, k] = acc
                for j in range(PANEL):
                    a = a - t[j, i] * left[j]
                    b = b - t[j, i] * right[j]
                nl.append(a); nr.append(b)
            if base + PANEL < MEMBERS:
                prod = outer_sum(tl, jnp.concatenate([tl, tr], axis=1))
                aug[base + PANEL:, :] = aug[base + PANEL:, :] - prod[base + PANEL:, :]
            left, right, s = nl, nr, ns

def finish(total_ref, x_ref, c_ref, o_ref, aug):
    total = total_ref[...]
    row = lax.broadcasted_iota(jnp.int32, (MEMBERS, MEMBERS), 0)
    col = lax.broadcasted_iota(jnp.int32, (MEMBERS, MEMBERS), 1)
    prior = float(MEMBERS - 1)
    unit = jnp.where(row == col, 1.0, 0.0)
    aug[:, :MEMBERS] = jnp.where(col >= row, total, 0.0) + prior * unit
    aug[:, MEMBERS:] = unit
    eliminate(aug)
    inverse = aug[:, MEMBERS:]
    lane = lax.broadcasted_iota(jnp.int32, (8, MEMBERS), 1)
    push = jnp.where(lane == MEMBERS - 1, jnp.broadcast_to(total[MEMBERS-2:MEMBERS-1, 0:1], (8, MEMBERS)), jnp.broadcast_to(total[MEMBERS-1:MEMBERS, :], (8, MEMBERS)))
    forward = lax.dot_general(push, inverse, (((1,), (1,)), ((), ())), precision=lax.Precision.HIGHEST, preferred_element_type=jnp.float32)
    mean_weights = jnp.dot(forward, inverse, precision=lax.Precision.HIGHEST, preferred_element_type=jnp.float32)
    weights = math.sqrt(prior) * inverse + mean_weights[0:1, :]
    for f in range(3):
        for r in range(2):
            k = 2 * f + r
            post = lax.dot_general(weights, x_ref[k * MEMBERS:(k + 1) * MEMBERS, :], (((1,), (1,)), ((), ())), precision=lax.Precision.HIGHEST, preferred_element_type=jnp.float32)
            o_ref[pl.ds(f * 2 * MEMBERS + r, MEMBERS, stride=2), :] = post + c_ref[k:k+1, :]


def turned(even_ref, prior_ref, state_ref, edge_ref, rows_ref):
    cols = MEMBERS
    even = even_ref[0:1, :] > 0.5
    for f in range(3):
        rows_ref[...] = prior_ref[2 * cols * f:2 * cols * (f + 1), :].astype(jnp.float32)
        for r in range(2):
            k = 2 * f + r
            block = rows_ref[pl.ds(r, cols, stride=2), :].T
            state_ref[k * cols:(k + 1) * cols, :] = block
            edge_ref[2 * k:2 * k + 2, :] = jnp.where(even, block[:2, :], block[cols - 2:, :])


def inner_edges(even_ref, state_ref, after_ref, edge_ref):
    cols = MEMBERS
    even = even_ref[0:1, :] > 0.5
    for k in range(6):
        low, high = state_ref[k * cols:k * cols + 2, :], state_ref[(k + 1) * cols - 2:(k + 1) * cols, :]
        edge_ref[2 * k:2 * k + 2, :] = jnp.where(even, high, low)


def row_of(state_ref, f, first):
    cols = MEMBERS
    low = state_ref[2 * f * cols:(2 * f + 1) * cols, :]
    high = state_ref[(2 * f + 1) * cols:(2 * f + 2) * cols, :]
    return jnp.where(first, low, high)


def early_rows(turn_ref, state_ref, out_ref):
    cols = MEMBERS
    first = turn_ref[6:7, :] < 0.5
    step = (2.0 * HALF_COURANT) * turn_ref[6:7, :] - HALF_COURANT
    spin = jnp.where(first, turn_ref[1:2, :], turn_ref[2:3, :])
    h, u, v = (row_of(state_ref, f, first) for f in range(3))
    out_ref[:cols, :] = h
    out_ref[cols:2 * cols, :] = v
    out_ref[2 * cols:, :] = v + step * row_of(state_ref, 0, ~first) - spin * u


def edge_rows(state_ref, west_ref, east_ref, wide, first, step):
    cols = MEMBERS

    def beside(ref, f, c):
        k = 4 * f + c
        return jnp.where(first, ref[k:k + 1, :], ref[k + 2:k + 3, :])

    wide[8:8 + cols, :] = row_of(state_ref, 1, first)
    wide[7:8, :] = beside(west_ref, 1, 1)
    wide[8 + cols:9 + cols, :] = beside(east_ref, 1, 0)
    slope = wide[9:9 + cols, :] - wide[7:7 + cols, :]
    mid = row_of(state_ref, 0, first) - HALF_COURANT * slope + step * row_of(state_ref, 2, ~first)
    return mid, beside(west_ref, 2, 1), beside(east_ref, 2, 0)


def late_rows(turn_ref, state_ref, west_ref, east_ref, out_ref, wide):
    cols = MEMBERS
    first = turn_ref[6:7, :] < 0.5
    step = (2.0 * HALF_COURANT) * turn_ref[6:7, :] - HALF_COURANT
    mid, west_v, east_v = edge_rows(state_ref, west_ref, east_ref, wide, first, step)
    out_ref[:cols, :] = mid
    out_ref[cols:cols + 1, :] = west_v
    out_ref[cols + 1:cols + 2, :] = east_v


def inner_rows(turn_ref, state_ref, west_ref, east_ref, after_ref, out_ref, wide):
    cols = MEMBERS
    first = turn_ref[6:7, :] > 0.5
    step = HALF_COURANT - (2.0 * HALF_COURANT) * turn_ref[6:7, :]
    spin = jnp.where(first, turn_ref[1:2, :], turn_ref[2:3, :])
    mid, west_v, east_v = edge_rows(state_ref, west_ref, east_ref, wide, first, step)
    h, u, v = (row_of(state_ref, f, first) for f in range(3))
    out_ref[:cols, :] = h
    out_ref[cols:2 * cols, :] = v
    out_ref[2 * cols:3 * cols, :] = v + step * row_of(state_ref, 0, ~first) - spin * u
    out_ref[3 * cols:4 * cols, :] = mid
    out_ref[4 * cols:4 * cols + 1, :] = west_v
    out_ref[4 * cols + 1:4 * cols + 2, :] = east_v


def assimilate(
    turn_ref, state_ref, west_ref, east_ref, early_ref, late_ref, inner_ref, weight_ref,
    sent_ref, anomaly_ref, center_ref, wide,
):
    a = HALF_COURANT
    cols = MEMBERS

    def field(f, r):
        k = 2 * f + r
        return state_ref[k * cols:(k + 1) * cols, :]

    def beside(ref, f, r, c):
        k = (2 * f + r) * 2 + c
        return ref[k:k + 1, :]

    def place(slot, block, low, high):
        wide[slot, 8:8 + cols, :] = block
        wide[slot, 7:8, :] = low
        wide[slot, 8 + cols:9 + cols, :] = high

    def slope(slot):
        return wide[slot, 9:9 + cols, :] - wide[slot, 7:7 + cols, :]

    spin = [turn_ref[1:2, :], turn_ref[2:3, :]]
    h = [field(0, 0), field(0, 1)]
    u = [field(1, 0), field(1, 1)]
    v = [field(2, 0), field(2, 1)]
    for r in range(2):
        place(4 + r, h[r], beside(west_ref, 0, r, 1), beside(east_ref, 0, r, 0))
        place(6 + r, u[r], beside(west_ref, 1, r, 1), beside(east_ref, 1, r, 0))
    even = turn_ref[6:7, :] < 0.5
    outer = [early_ref[k * cols:(k + 1) * cols, :] for k in range(3)] + [late_ref[:cols, :]]
    inner = [inner_ref[k * cols:(k + 1) * cols, :] for k in range(4)]
    outer += [late_ref[cols + k:cols + k + 1, :] for k in range(2)]
    inner += [inner_ref[4 * cols + k:4 * cols + k + 1, :] for k in range(2)]
    south_h, south_v, south_mid_v, south_mid_h, *south_edge = (
        jnp.where(even, o, i) for o, i in zip(outer, inner)
    )
    north_h, north_v, north_mid_v, north_mid_h, *north_edge = (
        jnp.where(even, i, o) for o, i in zip(outer, inner)
    )
    h_below, h_above = [south_h, h[0]], [h[1], north_h]
    v_below, v_above = [south_v, v[0]], [v[1], north_v]
    rate_h, rate_u, rate_v, mid_h, mid_u, mid_v = [], [], [], [], [], []
    for r in range(2):
        rate_h.append(-a * (slope(6 + r) + (v_above[r] - v_below[r])))
        rate_u.append(-a * slope(4 + r) + spin[r] * v[r])
        rate_v.append(-a * (h_above[r] - h_below[r]) - spin[r] * u[r])
        mid_h.append(h[r] + rate_h[r])
        mid_u.append(u[r] + rate_u[r])
        mid_v.append(v[r] + rate_v[r])
    for r in range(2):
        outside_h, outside_u = [], []
        for side, ref in enumerate((west_ref, east_ref)):
            near, far = (1, 0) if side == 0 else (0, 1)
            inner_h = h[r][0:1, :] if side == 0 else h[r][cols - 1:cols, :]
            inner_u = u[r][0:1, :] if side == 0 else u[r][cols - 1:cols, :]
            sign = -a if side == 0 else a
            own = [beside(ref, 2, 0, near), beside(ref, 2, 1, near)]
            below = south_edge[side] if r == 0 else own[0]
            above = own[1] if r == 0 else north_edge[side]
            outside_h.append(
                beside(ref, 0, r, near) + sign * (inner_u - beside(ref, 1, r, far)) - a * (above - below)
            )
            outside_u.append(
                beside(ref, 1, r, near) + sign * (inner_h - beside(ref, 0, r, far)) + spin[r] * own[r]
            )
        place(r, mid_h[r], *outside_h)
        place(2 + r, mid_u[r], *outside_u)
    has_south, has_north = turn_ref[4:5, :], turn_ref[5:6, :]
    south_mid_h = has_south * (south_mid_h - a * v[0])
    south_mid_v = has_south * (south_mid_v - a * h[0])
    north_mid_h = has_north * (north_mid_h + a * v[1])
    north_mid_v = has_north * (north_mid_v + a * h[1])
    mid_h_below, mid_h_above = [south_mid_h, mid_h[0]], [mid_h[1], north_mid_h]
    mid_v_below, mid_v_above = [south_mid_v, mid_v[0]], [mid_v[1], north_mid_v]
    forecast = [None] * 6
    for r in range(2):
        second_h = -a * (slope(2 + r) + (mid_v_above[r] - mid_v_below[r]))
        second_u = -a * slope(r) + spin[r] * mid_v[r]
        second_v = -a * (mid_h_above[r] - mid_h_below[r]) - spin[r] * mid_u[r]
        forecast[r] = h[r] + 0.5 * (rate_h[r] + second_h)
        forecast[2 + r] = u[r] + 0.5 * (rate_u[r] + second_u)
        forecast[4 + r] = v[r] + 0.5 * (rate_v[r] + second_v)
    share = jnp.full((8, MEMBERS), 1.0 / MEMBERS, jnp.float32)
    push = jnp.zeros((1, MEMBERS), jnp.float32)
    gram = jnp.zeros((MEMBERS, MEMBERS), jnp.float32)
    for k in range(6):
        mean = jnp.sum(forecast[k], axis=1, keepdims=True) * (1.0 / MEMBERS)
        anomaly = forecast[k] - mean
        anomaly_ref[k * cols:(k + 1) * cols, :] = anomaly
        row = lax.dot_general(
            share, forecast[k], (((1,), (1,)), ((), ())), precision=lax.Precision.HIGHEST,
            preferred_element_type=jnp.float32,
        )
        center_ref[k:k + 1, :] = row[0:1, :]
        weight = weight_ref[k * cols:(k + 1) * cols, 0:1]
        pull = weight_ref[k * cols:(k + 1) * cols, 1:2] - weight * mean
        push = push + jnp.sum(pull * anomaly, axis=0, keepdims=True)
        gram = gram + lax.dot_general(
            weight * anomaly, anomaly, (((0,), (0,)), ((), ())), precision=lax.Precision.HIGHEST,
            preferred_element_type=jnp.float32,
        )
    row_at = lax.broadcasted_iota(jnp.int32, (MEMBERS, MEMBERS), 0)
    col_at = lax.broadcasted_iota(jnp.int32, (MEMBERS, MEMBERS), 1)
    sent = jnp.where((row_at == MEMBERS - 1) & (col_at < MEMBERS - 1), push, gram)
    sent_ref[...] = jnp.where((row_at == MEMBERS - 2) & (col_at == 0), push[:, MEMBERS - 1:], sent)


def shards(prior_ensemble, observed, obs_error, obs_index, obs_count):
    a = HALF_COURANT
    members, rows, cols = prior_ensemble.shape[1:]
    entries = 3 * rows * cols
    lat_index, lon_index = lax.axis_index(LAT), lax.axis_index(LON)
    lat_count, lon_count = lax.axis_size(LAT), lax.axis_size(LON)
    lat_perms = pair_perms(lat_count, False)
    lon_perms = pair_perms(lon_count, True)
    lat_even, lon_even = lax.rem(lat_index, 2) == 0, lax.rem(lon_index, 2) == 0
    total_rows = rows * lat_count
    turn = rotation_at(lat_index * rows - 1 + jnp.arange(4, dtype=jnp.int32), total_rows)
    has_south = (lat_index > 0).astype(jnp.float32)
    has_north = (lat_index < lat_count - 1).astype(jnp.float32)

    vmem = pl.BlockSpec(memory_space=pltpu.VMEM)
    params = pltpu.CompilerParams(vmem_limit_bytes=16 * 1024 * 1024)
    small = pl.CostEstimate(flops=10**5, bytes_accessed=10**5, transcendentals=0)
    edges = 2 * 3 * rows

    def shaped(*heights):
        return [jax.ShapeDtypeStruct((height, members), jnp.float32) for height in heights]

    lon_flag = jnp.broadcast_to(lon_even.astype(jnp.float32), (8, members))
    state, outer_edge = pl.pallas_call(
        turned,
        in_specs=[vmem] * 2,
        out_specs=[vmem] * 2,
        out_shape=shaped(entries, edges),
        scratch_shapes=[pltpu.VMEM((rows * members, cols), jnp.float32)],
        compiler_params=params,
        cost_estimate=small,
    )(lon_flag, prior_ensemble.reshape(entries, cols))
    lon_inner, lon_outer = lon_perms
    outer_edge = lax.ppermute(outer_edge, LON, lon_outer)

    inner_perm, outer_perm = lat_perms
    edge_row = 1.0 - lat_even.astype(jnp.float32)
    scalars = jnp.concatenate([turn, jnp.stack([has_south, has_north, edge_row, edge_row])])
    scalars = jnp.broadcast_to(scalars[:, None], (8, members))
    early = pl.pallas_call(
        early_rows, in_specs=[vmem] * 2, out_specs=vmem, out_shape=shaped(3 * cols)[0],
        compiler_params=params, cost_estimate=small,
    )(scalars, state)
    outer_early = lax.ppermute(early, LAT, outer_perm)

    inner_edge = pl.pallas_call(
        inner_edges, in_specs=[vmem] * 3, out_specs=vmem, out_shape=shaped(edges)[0],
        compiler_params=params, cost_estimate=small,
    )(lon_flag, state, early)
    inner_edge = lax.ppermute(inner_edge, LON, lon_inner)
    west = jnp.where(lon_even, outer_edge, inner_edge)
    east = jnp.where(lon_even, inner_edge, outer_edge)

    wide_row = [pltpu.VMEM((cols + 16, members), jnp.float32)]
    late = pl.pallas_call(
        late_rows, in_specs=[vmem] * 4, out_specs=vmem, out_shape=shaped(cols + 2)[0],
        scratch_shapes=wide_row, compiler_params=params, cost_estimate=small,
    )(scalars, state, west, east)
    outer_late = lax.ppermute(late, LAT, outer_perm)
    inner = pl.pallas_call(
        inner_rows, in_specs=[vmem] * 5, out_specs=vmem, out_shape=shaped(4 * cols + 2)[0],
        scratch_shapes=wide_row, compiler_params=params, cost_estimate=small,
    )(scalars, state, west, east, late)
    inner = lax.ppermute(inner, LAT, inner_perm)

    index = obs_index.reshape(-1)
    slots = index.shape[0]
    live = (jnp.arange(slots, dtype=jnp.int32) < obs_count.reshape(())).astype(jnp.float32)
    weight = live / obs_error.reshape(-1)
    weight = weight * weight
    named = (jnp.arange(entries, dtype=jnp.int32)[:, None] == index[None, :]).astype(jnp.float32)
    weights = jnp.dot(
        named, jnp.stack([weight, weight * observed.reshape(-1)], axis=1), precision=lax.Precision.HIGHEST
    )
    sent, anomaly, center = pl.pallas_call(
        assimilate,
        in_specs=[vmem] * 8,
        out_specs=[vmem] * 3,
        out_shape=[
            jax.ShapeDtypeStruct((members, members), jnp.float32),
            jax.ShapeDtypeStruct((entries, members), jnp.float32),
            jax.ShapeDtypeStruct((3 * rows, cols), jnp.float32),
        ],
        scratch_shapes=[pltpu.VMEM((8, cols + 16, members), jnp.float32)],
        compiler_params=params,
        cost_estimate=pl.CostEstimate(flops=3 * 10**7, bytes_accessed=2 * 10**6, transcendentals=0),
    )(
        scalars, state, west, east, outer_early, outer_late, inner, weights,
    )
    total = all_sum(sent)
    posterior = pl.pallas_call(
        finish,
        out_shape=jax.ShapeDtypeStruct((entries, cols), jnp.float32),
        scratch_shapes=[pltpu.VMEM((members, 2 * members), jnp.float32)],
        compiler_params=params,
        cost_estimate=pl.CostEstimate(flops=3 * 10**7, bytes_accessed=10**6, transcendentals=0),
    )(total, anomaly, center)
    return posterior.reshape(3, members, rows, cols)


def solution(mesh):
    lat, lon = mesh.shape["lat"], mesh.shape["lon"]
    parts = Mesh(mesh.devices.reshape(lat // 4, 2, 2, lon // 4, 4), LAT + LON)
    placed = (
        P(None, None, LAT, LON),
        P(LAT, LON, None),
        P(LAT, LON, None),
        P(LAT, LON, None),
        P(LAT, LON),
    )
    return jax.shard_map(
        shards, mesh=parts, in_specs=placed, out_specs=P(None, None, LAT, LON), check_vma=False
    )
```

```python
import math

import jax
import jax.numpy as jnp
from jax import lax
from jax.experimental import pallas as pl
from jax.experimental.pallas import tpu as pltpu
from jax.sharding import Mesh, PartitionSpec as P

HALF_COURANT = 0.4
ROTATION = 0.8
BAND = math.pi / 6.0
LAT = ("x", "zh", "core")
LON = ("zl", "y")
PLANE = ("x", "core", "y")
LINE = ("zh", "zl")
MEMBERS = 128
PANEL = 8


def rotation_at(rows, total_rows):
    latitude = BAND * (2.0 * (rows.astype(jnp.float32) + 0.5) / total_rows - 1.0)
    return ROTATION * jnp.sin(latitude)


def pair_perms(count, periodic):
    inner = [(i, i ^ 1) for i in range(count)]
    outer = []
    for i in range(1, count, 2):
        if i + 1 < count or periodic:
            j = (i + 1) % count
            outer += [(i, j), (j, i)]
    return inner, outer


def all_sum(block):
    plane = lax.axis_size(PLANE)
    line = lax.axis_size(LINE)
    rows, cols = block.shape
    part = rows // plane
    mine = lax.all_to_all(block.reshape(plane, part, cols), PLANE, 0, 0, tiled=True).sum(0)
    mine = lax.all_to_all(
        jnp.broadcast_to(mine[None], (line, part, cols)), LINE, 0, 0, tiled=True
    ).sum(0)
    whole = lax.all_to_all(
        jnp.broadcast_to(mine[None], (plane, part, cols)), PLANE, 0, 0, tiled=True
    )
    return whole.reshape(rows, cols)


def splat(tile, lane):
    return jnp.broadcast_to(tile[:, lane:lane + 1], tile.shape)

def thirds(x):
    hi = x.astype(jnp.bfloat16).astype(jnp.float32)
    rest = x - hi
    mid = rest.astype(jnp.bfloat16).astype(jnp.float32)
    return hi, mid, rest - mid

def outer_sum(left, whole):
    a, b, c = thirds(left)
    d, e, f = thirds(whole)
    first = jnp.concatenate([a, a, b, a, c, b], axis=0).astype(jnp.bfloat16)
    second = jnp.concatenate([d, e, d, f, d, e], axis=0).astype(jnp.bfloat16)
    return lax.dot_general(first, second, (((0,), (0,)), ((), ())), preferred_element_type=jnp.float32)

def eliminate(aug):
    sub = lax.broadcasted_iota(jnp.int32, (PANEL, MEMBERS), 0)
    def fetch(i):
        return (jnp.broadcast_to(aug[i:i+1, :MEMBERS], (PANEL, MEMBERS)), jnp.broadcast_to(aug[i:i+1, MEMBERS:], (PANEL, MEMBERS)))
    left, right = zip(*[fetch(i) for i in range(PANEL)])
    left, right = list(left), list(right)
    s = {(i, k): splat(left[i], k) for i in range(PANEL) for k in range(i, PANEL)}
    for p in range(MEMBERS // PANEL):
        for j in range(PANEL):
            r = lax.rsqrt(s[j, j])
            left[j] = left[j] * r
            right[j] = right[j] * r
            l = {i: s[j, i] * r for i in range(j + 1, PANEL)}
            for i in range(j + 1, PANEL):
                for k in range(i, PANEL):
                    s[i, k] = s[i, k] - l[i] * l[k]
                left[i] = left[i] - l[i] * left[j]
                right[i] = right[i] - l[i] * right[j]
        tl, tr = left[0], right[0]
        for j in range(1, PANEL):
            tl = jnp.where(sub == j, left[j], tl)
            tr = jnp.where(sub == j, right[j], tr)
        aug[p*PANEL:(p+1)*PANEL, MEMBERS:] = tr
        q = p + 1
        if q * PANEL < MEMBERS:
            base = q * PANEL
            t = {(j, i): splat(left[j], base + i) for j in range(PANEL) for i in range(PANEL)}
            nl, nr, ns = [], [], {}
            for i in range(PANEL):
                a, b = fetch(base + i)
                for k in range(i, PANEL):
                    acc = splat(a, base + k)
                    for j in range(PANEL):
                        acc = acc - t[j, i] * t[j, k]
                    ns[i, k] = acc
                for j in range(PANEL):
                    a = a - t[j, i] * left[j]
                    b = b - t[j, i] * right[j]
                nl.append(a); nr.append(b)
            if base + PANEL < MEMBERS:
                prod = outer_sum(tl, jnp.concatenate([tl, tr], axis=1))
                aug[base + PANEL:, :] = aug[base + PANEL:, :] - prod[base + PANEL:, :]
            left, right, s = nl, nr, ns

def finish(total_ref, x_ref, c_ref, o_ref, aug):
    total = total_ref[...]
    row = lax.broadcasted_iota(jnp.int32, (MEMBERS, MEMBERS), 0)
    col = lax.broadcasted_iota(jnp.int32, (MEMBERS, MEMBERS), 1)
    prior = float(MEMBERS - 1)
    unit = jnp.where(row == col, 1.0, 0.0)
    aug[:, :MEMBERS] = jnp.where(col >= row, total, 0.0) + prior * unit
    aug[:, MEMBERS:] = unit
    eliminate(aug)
    inverse = aug[:, MEMBERS:]
    lane = lax.broadcasted_iota(jnp.int32, (8, MEMBERS), 1)
    push = jnp.where(lane == MEMBERS - 1, jnp.broadcast_to(total[MEMBERS-2:MEMBERS-1, 0:1], (8, MEMBERS)), jnp.broadcast_to(total[MEMBERS-1:MEMBERS, :], (8, MEMBERS)))
    forward = lax.dot_general(push, inverse, (((1,), (1,)), ((), ())), precision=lax.Precision.HIGHEST, preferred_element_type=jnp.float32)
    mean_weights = jnp.dot(forward, inverse, precision=lax.Precision.HIGHEST, preferred_element_type=jnp.float32)
    weights = math.sqrt(prior) * inverse + mean_weights[0:1, :]
    for f in range(3):
        post = lax.dot_general(
            weights, x_ref[2 * f * MEMBERS:2 * (f + 1) * MEMBERS, :], (((1,), (1,)), ((), ())),
            precision=lax.Precision.HIGHEST, preferred_element_type=jnp.float32,
        )
        for r in range(2):
            center = c_ref[2 * f + r:2 * f + r + 1, :]
            o_ref[pl.ds(2 * f * MEMBERS + r, MEMBERS, stride=2), :] = post[:, r * MEMBERS:(r + 1) * MEMBERS] + center


def turned(even_ref, prior_ref, state_ref, edge_ref, rows_ref):
    cols = MEMBERS
    even = even_ref[0:1, :] > 0.5
    for f in range(3):
        rows_ref[...] = prior_ref[2 * cols * f:2 * cols * (f + 1), :].astype(jnp.float32)
        for r in range(2):
            k = 2 * f + r
            block = rows_ref[pl.ds(r, cols, stride=2), :].T
            state_ref[k * cols:(k + 1) * cols, :] = block
            edge_ref[2 * k:2 * k + 2, :] = jnp.where(even, block[:2, :], block[cols - 2:, :])


def inner_edges(even_ref, state_ref, after_ref, edge_ref):
    cols = MEMBERS
    even = even_ref[0:1, :] > 0.5
    for k in range(6):
        low, high = state_ref[k * cols:k * cols + 2, :], state_ref[(k + 1) * cols - 2:(k + 1) * cols, :]
        edge_ref[2 * k:2 * k + 2, :] = jnp.where(even, high, low)


def row_of(state_ref, f, first):
    cols = MEMBERS
    low = state_ref[2 * f * cols:(2 * f + 1) * cols, :]
    high = state_ref[(2 * f + 1) * cols:(2 * f + 2) * cols, :]
    return jnp.where(first, low, high)


def early_rows(turn_ref, state_ref, out_ref):
    cols = MEMBERS
    first = turn_ref[6:7, :] < 0.5
    step = (2.0 * HALF_COURANT) * turn_ref[6:7, :] - HALF_COURANT
    spin = jnp.where(first, turn_ref[1:2, :], turn_ref[2:3, :])
    h, u, v = (row_of(state_ref, f, first) for f in range(3))
    out_ref[:cols, :] = h
    out_ref[cols:2 * cols, :] = v
    out_ref[2 * cols:, :] = v + step * row_of(state_ref, 0, ~first) - spin * u


def edge_rows(state_ref, west_ref, east_ref, wide, first, step):
    cols = MEMBERS

    def beside(ref, f, c):
        k = 4 * f + c
        return jnp.where(first, ref[k:k + 1, :], ref[k + 2:k + 3, :])

    wide[8:8 + cols, :] = row_of(state_ref, 1, first)
    wide[7:8, :] = beside(west_ref, 1, 1)
    wide[8 + cols:9 + cols, :] = beside(east_ref, 1, 0)
    slope = wide[9:9 + cols, :] - wide[7:7 + cols, :]
    mid = row_of(state_ref, 0, first) - HALF_COURANT * slope + step * row_of(state_ref, 2, ~first)
    return mid, beside(west_ref, 2, 1), beside(east_ref, 2, 0)


def late_rows(turn_ref, state_ref, west_ref, east_ref, out_ref, wide):
    cols = MEMBERS
    first = turn_ref[6:7, :] < 0.5
    step = (2.0 * HALF_COURANT) * turn_ref[6:7, :] - HALF_COURANT
    mid, west_v, east_v = edge_rows(state_ref, west_ref, east_ref, wide, first, step)
    out_ref[:cols, :] = mid
    out_ref[cols:cols + 1, :] = west_v
    out_ref[cols + 1:cols + 2, :] = east_v


def inner_rows(turn_ref, state_ref, west_ref, east_ref, after_ref, out_ref, wide):
    cols = MEMBERS
    first = turn_ref[6:7, :] > 0.5
    step = HALF_COURANT - (2.0 * HALF_COURANT) * turn_ref[6:7, :]
    spin = jnp.where(first, turn_ref[1:2, :], turn_ref[2:3, :])
    mid, west_v, east_v = edge_rows(state_ref, west_ref, east_ref, wide, first, step)
    h, u, v = (row_of(state_ref, f, first) for f in range(3))
    out_ref[:cols, :] = h
    out_ref[cols:2 * cols, :] = v
    out_ref[2 * cols:3 * cols, :] = v + step * row_of(state_ref, 0, ~first) - spin * u
    out_ref[3 * cols:4 * cols, :] = mid
    out_ref[4 * cols:4 * cols + 1, :] = west_v
    out_ref[4 * cols + 1:4 * cols + 2, :] = east_v


def assimilate(
    turn_ref, state_ref, west_ref, east_ref, early_ref, late_ref, inner_ref, weight_ref,
    sent_ref, anomaly_ref, center_ref, wide,
):
    a = HALF_COURANT
    cols = MEMBERS

    def field(f, r):
        k = 2 * f + r
        return state_ref[k * cols:(k + 1) * cols, :]

    def beside(ref, f, r, c):
        k = (2 * f + r) * 2 + c
        return ref[k:k + 1, :]

    def place(slot, block, low, high):
        wide[slot, 8:8 + cols, :] = block
        wide[slot, 7:8, :] = low
        wide[slot, 8 + cols:9 + cols, :] = high

    def slope(slot):
        return wide[slot, 9:9 + cols, :] - wide[slot, 7:7 + cols, :]

    spin = [turn_ref[1:2, :], turn_ref[2:3, :]]
    h = [field(0, 0), field(0, 1)]
    u = [field(1, 0), field(1, 1)]
    v = [field(2, 0), field(2, 1)]
    for r in range(2):
        place(4 + r, h[r], beside(west_ref, 0, r, 1), beside(east_ref, 0, r, 0))
        place(6 + r, u[r], beside(west_ref, 1, r, 1), beside(east_ref, 1, r, 0))
    even = turn_ref[6:7, :] < 0.5
    outer = [early_ref[k * cols:(k + 1) * cols, :] for k in range(3)] + [late_ref[:cols, :]]
    inner = [inner_ref[k * cols:(k + 1) * cols, :] for k in range(4)]
    outer += [late_ref[cols + k:cols + k + 1, :] for k in range(2)]
    inner += [inner_ref[4 * cols + k:4 * cols + k + 1, :] for k in range(2)]
    south_h, south_v, south_mid_v, south_mid_h, *south_edge = (
        jnp.where(even, o, i) for o, i in zip(outer, inner)
    )
    north_h, north_v, north_mid_v, north_mid_h, *north_edge = (
        jnp.where(even, i, o) for o, i in zip(outer, inner)
    )
    h_below, h_above = [south_h, h[0]], [h[1], north_h]
    v_below, v_above = [south_v, v[0]], [v[1], north_v]
    rate_h, rate_u, rate_v, mid_h, mid_u, mid_v = [], [], [], [], [], []
    for r in range(2):
        rate_h.append(-a * (slope(6 + r) + (v_above[r] - v_below[r])))
        rate_u.append(-a * slope(4 + r) + spin[r] * v[r])
        rate_v.append(-a * (h_above[r] - h_below[r]) - spin[r] * u[r])
        mid_h.append(h[r] + rate_h[r])
        mid_u.append(u[r] + rate_u[r])
        mid_v.append(v[r] + rate_v[r])
    for r in range(2):
        outside_h, outside_u = [], []
        for side, ref in enumerate((west_ref, east_ref)):
            near, far = (1, 0) if side == 0 else (0, 1)
            inner_h = h[r][0:1, :] if side == 0 else h[r][cols - 1:cols, :]
            inner_u = u[r][0:1, :] if side == 0 else u[r][cols - 1:cols, :]
            sign = -a if side == 0 else a
            own = [beside(ref, 2, 0, near), beside(ref, 2, 1, near)]
            below = south_edge[side] if r == 0 else own[0]
            above = own[1] if r == 0 else north_edge[side]
            outside_h.append(
                beside(ref, 0, r, near) + sign * (inner_u - beside(ref, 1, r, far)) - a * (above - below)
            )
            outside_u.append(
                beside(ref, 1, r, near) + sign * (inner_h - beside(ref, 0, r, far)) + spin[r] * own[r]
            )
        place(r, mid_h[r], *outside_h)
        place(2 + r, mid_u[r], *outside_u)
    has_south, has_north = turn_ref[4:5, :], turn_ref[5:6, :]
    south_mid_h = has_south * (south_mid_h - a * v[0])
    south_mid_v = has_south * (south_mid_v - a * h[0])
    north_mid_h = has_north * (north_mid_h + a * v[1])
    north_mid_v = has_north * (north_mid_v + a * h[1])
    mid_h_below, mid_h_above = [south_mid_h, mid_h[0]], [mid_h[1], north_mid_h]
    mid_v_below, mid_v_above = [south_mid_v, mid_v[0]], [mid_v[1], north_mid_v]
    forecast = [None] * 6
    for r in range(2):
        second_h = -a * (slope(2 + r) + (mid_v_above[r] - mid_v_below[r]))
        second_u = -a * slope(r) + spin[r] * mid_v[r]
        second_v = -a * (mid_h_above[r] - mid_h_below[r]) - spin[r] * mid_u[r]
        forecast[r] = h[r] + 0.5 * (rate_h[r] + second_h)
        forecast[2 + r] = u[r] + 0.5 * (rate_u[r] + second_u)
        forecast[4 + r] = v[r] + 0.5 * (rate_v[r] + second_v)
    share = jnp.full((8, MEMBERS), 1.0 / MEMBERS, jnp.float32)
    push = jnp.zeros((1, MEMBERS), jnp.float32)
    anomalies, weighted = [], []
    for k in range(6):
        mean = jnp.sum(forecast[k], axis=1, keepdims=True) * (1.0 / MEMBERS)
        anomaly = forecast[k] - mean
        anomaly_ref[k * cols:(k + 1) * cols, :] = anomaly
        row = lax.dot_general(
            share, forecast[k], (((1,), (1,)), ((), ())), precision=lax.Precision.HIGHEST,
            preferred_element_type=jnp.float32,
        )
        center_ref[k:k + 1, :] = row[0:1, :]
        weight = weight_ref[k * cols:(k + 1) * cols, 0:1]
        pull = weight_ref[k * cols:(k + 1) * cols, 1:2] - weight * mean
        push = push + jnp.sum(pull * anomaly, axis=0, keepdims=True)
        anomalies.append(anomaly)
        weighted.append(weight * anomaly)
    gram = lax.dot_general(
        jnp.concatenate(weighted, axis=0), jnp.concatenate(anomalies, axis=0), (((0,), (0,)), ((), ())),
        precision=lax.Precision.HIGHEST, preferred_element_type=jnp.float32,
    )
    row_at = lax.broadcasted_iota(jnp.int32, (MEMBERS, MEMBERS), 0)
    col_at = lax.broadcasted_iota(jnp.int32, (MEMBERS, MEMBERS), 1)
    sent = jnp.where((row_at == MEMBERS - 1) & (col_at < MEMBERS - 1), push, gram)
    sent_ref[...] = jnp.where((row_at == MEMBERS - 2) & (col_at == 0), push[:, MEMBERS - 1:], sent)


def shards(prior_ensemble, observed, obs_error, obs_index, obs_count):
    a = HALF_COURANT
    members, rows, cols = prior_ensemble.shape[1:]
    entries = 3 * rows * cols
    lat_index, lon_index = lax.axis_index(LAT), lax.axis_index(LON)
    lat_count, lon_count = lax.axis_size(LAT), lax.axis_size(LON)
    lat_perms = pair_perms(lat_count, False)
    lon_perms = pair_perms(lon_count, True)
    lat_even, lon_even = lax.rem(lat_index, 2) == 0, lax.rem(lon_index, 2) == 0
    total_rows = rows * lat_count
    turn = rotation_at(lat_index * rows - 1 + jnp.arange(4, dtype=jnp.int32), total_rows)
    has_south = (lat_index > 0).astype(jnp.float32)
    has_north = (lat_index < lat_count - 1).astype(jnp.float32)

    vmem = pl.BlockSpec(memory_space=pltpu.VMEM)
    params = pltpu.CompilerParams(vmem_limit_bytes=16 * 1024 * 1024)
    small = pl.CostEstimate(flops=10**5, bytes_accessed=10**5, transcendentals=0)
    edges = 2 * 3 * rows

    def shaped(*heights):
        return [jax.ShapeDtypeStruct((height, members), jnp.float32) for height in heights]

    lon_flag = jnp.broadcast_to(lon_even.astype(jnp.float32), (8, members))
    state, outer_edge = pl.pallas_call(
        turned,
        in_specs=[vmem] * 2,
        out_specs=[vmem] * 2,
        out_shape=shaped(entries, edges),
        scratch_shapes=[pltpu.VMEM((rows * members, cols), jnp.float32)],
        compiler_params=params,
        cost_estimate=small,
    )(lon_flag, prior_ensemble.reshape(entries, cols))
    lon_inner, lon_outer = lon_perms
    outer_edge = lax.ppermute(outer_edge, LON, lon_outer)

    inner_perm, outer_perm = lat_perms
    edge_row = 1.0 - lat_even.astype(jnp.float32)
    scalars = jnp.concatenate([turn, jnp.stack([has_south, has_north, edge_row, edge_row])])
    scalars = jnp.broadcast_to(scalars[:, None], (8, members))
    early = pl.pallas_call(
        early_rows, in_specs=[vmem] * 2, out_specs=vmem, out_shape=shaped(3 * cols)[0],
        compiler_params=params, cost_estimate=small,
    )(scalars, state)
    outer_early = lax.ppermute(early, LAT, outer_perm)

    inner_edge = pl.pallas_call(
        inner_edges, in_specs=[vmem] * 3, out_specs=vmem, out_shape=shaped(edges)[0],
        compiler_params=params, cost_estimate=small,
    )(lon_flag, state, early)
    inner_edge = lax.ppermute(inner_edge, LON, lon_inner)
    west = jnp.where(lon_even, outer_edge, inner_edge)
    east = jnp.where(lon_even, inner_edge, outer_edge)

    wide_row = [pltpu.VMEM((cols + 16, members), jnp.float32)]
    late = pl.pallas_call(
        late_rows, in_specs=[vmem] * 4, out_specs=vmem, out_shape=shaped(cols + 2)[0],
        scratch_shapes=wide_row, compiler_params=params, cost_estimate=small,
    )(scalars, state, west, east)
    outer_late = lax.ppermute(late, LAT, outer_perm)
    inner = pl.pallas_call(
        inner_rows, in_specs=[vmem] * 5, out_specs=vmem, out_shape=shaped(4 * cols + 2)[0],
        scratch_shapes=wide_row, compiler_params=params, cost_estimate=small,
    )(scalars, state, west, east, late)
    inner = lax.ppermute(inner, LAT, inner_perm)

    index = obs_index.reshape(-1)
    slots = index.shape[0]
    live = (jnp.arange(slots, dtype=jnp.int32) < obs_count.reshape(())).astype(jnp.float32)
    weight = live / obs_error.reshape(-1)
    weight = weight * weight
    named = (jnp.arange(entries, dtype=jnp.int32)[:, None] == index[None, :]).astype(jnp.float32)
    weights = jnp.dot(
        named, jnp.stack([weight, weight * observed.reshape(-1)], axis=1), precision=lax.Precision.HIGHEST
    )
    sent, anomaly, center = pl.pallas_call(
        assimilate,
        in_specs=[vmem] * 8,
        out_specs=[vmem] * 3,
        out_shape=[
            jax.ShapeDtypeStruct((members, members), jnp.float32),
            jax.ShapeDtypeStruct((entries, members), jnp.float32),
            jax.ShapeDtypeStruct((3 * rows, cols), jnp.float32),
        ],
        scratch_shapes=[pltpu.VMEM((8, cols + 16, members), jnp.float32)],
        compiler_params=params,
        cost_estimate=pl.CostEstimate(flops=3 * 10**7, bytes_accessed=2 * 10**6, transcendentals=0),
    )(
        scalars, state, west, east, outer_early, outer_late, inner, weights,
    )
    total = all_sum(sent)
    posterior = pl.pallas_call(
        finish,
        out_shape=jax.ShapeDtypeStruct((entries, cols), jnp.float32),
        scratch_shapes=[pltpu.VMEM((members, 2 * members), jnp.float32)],
        compiler_params=params,
        cost_estimate=pl.CostEstimate(flops=3 * 10**7, bytes_accessed=10**6, transcendentals=0),
    )(total, anomaly, center)
    return posterior.reshape(3, members, rows, cols)


def solution(mesh):
    lat, lon = mesh.shape["lat"], mesh.shape["lon"]
    parts = Mesh(mesh.devices.reshape(lat // 4, 2, 2, lon // 4, 4), LAT + LON)
    placed = (
        P(None, None, LAT, LON),
        P(LAT, LON, None),
        P(LAT, LON, None),
        P(LAT, LON, None),
        P(LAT, LON),
    )
    return jax.shard_map(
        shards, mesh=parts, in_specs=placed, out_specs=P(None, None, LAT, LON), check_vma=False
    )
```

```python
import math

import jax
import jax.numpy as jnp
from jax import lax
from jax.experimental import pallas as pl
from jax.experimental.pallas import tpu as pltpu
from jax.sharding import Mesh, PartitionSpec as P

HALF_COURANT = 0.4
ROTATION = 0.8
BAND = math.pi / 6.0
LAT = ("x", "zh", "core")
LON = ("zl", "y")
PLANE = ("x", "core", "y")
LINE = ("zh", "zl")
MEMBERS = 128
PANEL = 8


def rotation_at(rows, total_rows):
    latitude = BAND * (2.0 * (rows.astype(jnp.float32) + 0.5) / total_rows - 1.0)
    return ROTATION * jnp.sin(latitude)


def pair_perms(count, periodic):
    inner = [(i, i ^ 1) for i in range(count)]
    outer = []
    for i in range(1, count, 2):
        if i + 1 < count or periodic:
            j = (i + 1) % count
            outer += [(i, j), (j, i)]
    return inner, outer


def all_sum(block):
    plane = lax.axis_size(PLANE)
    line = lax.axis_size(LINE)
    rows, cols = block.shape
    part = rows // plane
    mine = lax.all_to_all(block.reshape(plane, part, cols), PLANE, 0, 0, tiled=True).sum(0)
    mine = lax.all_to_all(
        jnp.broadcast_to(mine[None], (line, part, cols)), LINE, 0, 0, tiled=True
    ).sum(0)
    whole = lax.all_to_all(
        jnp.broadcast_to(mine[None], (plane, part, cols)), PLANE, 0, 0, tiled=True
    )
    return whole.reshape(rows, cols)


def splat(tile, lane):
    return jnp.broadcast_to(tile[:, lane:lane + 1], tile.shape)

def thirds(x):
    hi = x.astype(jnp.bfloat16).astype(jnp.float32)
    rest = x - hi
    mid = rest.astype(jnp.bfloat16).astype(jnp.float32)
    return hi, mid, rest - mid

def outer_sum(left, whole):
    a, b, c = thirds(left)
    d, e, f = thirds(whole)
    first = jnp.concatenate([a, a, b, a, c, b], axis=0).astype(jnp.bfloat16)
    second = jnp.concatenate([d, e, d, f, d, e], axis=0).astype(jnp.bfloat16)
    return lax.dot_general(first, second, (((0,), (0,)), ((), ())), preferred_element_type=jnp.float32)

def eliminate(aug):
    sub = lax.broadcasted_iota(jnp.int32, (PANEL, MEMBERS), 0)
    def fetch(i):
        return (jnp.broadcast_to(aug[i:i+1, :MEMBERS], (PANEL, MEMBERS)), jnp.broadcast_to(aug[i:i+1, MEMBERS:], (PANEL, MEMBERS)))
    left, right = zip(*[fetch(i) for i in range(PANEL)])
    left, right = list(left), list(right)
    s = {(i, k): splat(left[i], k) for i in range(PANEL) for k in range(i, PANEL)}
    for p in range(MEMBERS // PANEL):
        for j in range(PANEL):
            r = lax.rsqrt(s[j, j])
            left[j] = left[j] * r
            right[j] = right[j] * r
            l = {i: s[j, i] * r for i in range(j + 1, PANEL)}
            for i in range(j + 1, PANEL):
                for k in range(i, PANEL):
                    s[i, k] = s[i, k] - l[i] * l[k]
                left[i] = left[i] - l[i] * left[j]
                right[i] = right[i] - l[i] * right[j]
        tl, tr = left[0], right[0]
        for j in range(1, PANEL):
            tl = jnp.where(sub == j, left[j], tl)
            tr = jnp.where(sub == j, right[j], tr)
        aug[p*PANEL:(p+1)*PANEL, MEMBERS:] = tr
        q = p + 1
        if q * PANEL < MEMBERS:
            base = q * PANEL
            t = {(j, i): splat(left[j], base + i) for j in range(PANEL) for i in range(PANEL)}
            nl, nr, ns = [], [], {}
            for i in range(PANEL):
                a, b = fetch(base + i)
                for k in range(i, PANEL):
                    acc = splat(a, base + k)
                    for j in range(PANEL):
                        acc = acc - t[j, i] * t[j, k]
                    ns[i, k] = acc
                for j in range(PANEL):
                    a = a - t[j, i] * left[j]
                    b = b - t[j, i] * right[j]
                nl.append(a); nr.append(b)
            if base + PANEL < MEMBERS:
                prod = outer_sum(tl, jnp.concatenate([tl, tr], axis=1))
                aug[base + PANEL:, :] = aug[base + PANEL:, :] - prod[base + PANEL:, :]
            left, right, s = nl, nr, ns

def finish(total_ref, x_ref, c_ref, o_ref, aug):
    total = total_ref[...]
    row = lax.broadcasted_iota(jnp.int32, (MEMBERS, MEMBERS), 0)
    col = lax.broadcasted_iota(jnp.int32, (MEMBERS, MEMBERS), 1)
    prior = float(MEMBERS - 1)
    unit = jnp.where(row == col, 1.0, 0.0)
    aug[:, :MEMBERS] = jnp.where(col >= row, total, 0.0) + prior * unit
    aug[:, MEMBERS:] = unit
    eliminate(aug)
    inverse = aug[:, MEMBERS:]
    lane = lax.broadcasted_iota(jnp.int32, (8, MEMBERS), 1)
    push = jnp.where(lane == MEMBERS - 1, jnp.broadcast_to(total[MEMBERS-2:MEMBERS-1, 0:1], (8, MEMBERS)), jnp.broadcast_to(total[MEMBERS-1:MEMBERS, :], (8, MEMBERS)))
    forward = lax.dot_general(push, inverse, (((1,), (1,)), ((), ())), precision=lax.Precision.HIGHEST, preferred_element_type=jnp.float32)
    mean_weights = jnp.dot(forward, inverse, precision=lax.Precision.HIGHEST, preferred_element_type=jnp.float32)
    weights = math.sqrt(prior) * inverse + mean_weights[0:1, :]
    for f in range(3):
        post = lax.dot_general(
            weights, x_ref[2 * f * MEMBERS:2 * (f + 1) * MEMBERS, :], (((1,), (1,)), ((), ())),
            precision=lax.Precision.HIGHEST, preferred_element_type=jnp.float32,
        )
        for r in range(2):
            center = c_ref[2 * f + r:2 * f + r + 1, :]
            o_ref[pl.ds(2 * f * MEMBERS + r, MEMBERS, stride=2), :] = post[:, r * MEMBERS:(r + 1) * MEMBERS] + center


def turned(even_ref, prior_ref, state_ref, edge_ref, rows_ref):
    cols = MEMBERS
    even = even_ref[0:1, :] > 0.5
    for f in range(3):
        rows_ref[...] = prior_ref[2 * cols * f:2 * cols * (f + 1), :].astype(jnp.float32)
        for r in range(2):
            k = 2 * f + r
            block = rows_ref[pl.ds(r, cols, stride=2), :].T
            state_ref[k * cols:(k + 1) * cols, :] = block
            edge_ref[2 * k:2 * k + 2, :] = jnp.where(even, block[:2, :], block[cols - 2:, :])


def inner_edges(even_ref, state_ref, after_ref, edge_ref):
    cols = MEMBERS
    even = even_ref[0:1, :] > 0.5
    for k in range(6):
        low, high = state_ref[k * cols:k * cols + 2, :], state_ref[(k + 1) * cols - 2:(k + 1) * cols, :]
        edge_ref[2 * k:2 * k + 2, :] = jnp.where(even, high, low)


def row_of(state_ref, f, first):
    cols = MEMBERS
    low = state_ref[2 * f * cols:(2 * f + 1) * cols, :]
    high = state_ref[(2 * f + 1) * cols:(2 * f + 2) * cols, :]
    return jnp.where(first, low, high)


def early_rows(turn_ref, state_ref, out_ref):
    cols = MEMBERS
    first = turn_ref[6:7, :] < 0.5
    step = (2.0 * HALF_COURANT) * turn_ref[6:7, :] - HALF_COURANT
    spin = jnp.where(first, turn_ref[1:2, :], turn_ref[2:3, :])
    h, u, v = (row_of(state_ref, f, first) for f in range(3))
    out_ref[:cols, :] = h
    out_ref[cols:2 * cols, :] = v
    out_ref[2 * cols:, :] = v + step * row_of(state_ref, 0, ~first) - spin * u


def edge_rows(state_ref, west_ref, east_ref, wide, first, step):
    cols = MEMBERS

    def beside(ref, f, c):
        k = 4 * f + c
        return jnp.where(first, ref[k:k + 1, :], ref[k + 2:k + 3, :])

    wide[8:8 + cols, :] = row_of(state_ref, 1, first)
    wide[7:8, :] = beside(west_ref, 1, 1)
    wide[8 + cols:9 + cols, :] = beside(east_ref, 1, 0)
    slope = wide[9:9 + cols, :] - wide[7:7 + cols, :]
    mid = row_of(state_ref, 0, first) - HALF_COURANT * slope + step * row_of(state_ref, 2, ~first)
    return mid, beside(west_ref, 2, 1), beside(east_ref, 2, 0)


def late_rows(turn_ref, state_ref, west_ref, east_ref, out_ref, wide):
    cols = MEMBERS
    first = turn_ref[6:7, :] < 0.5
    step = (2.0 * HALF_COURANT) * turn_ref[6:7, :] - HALF_COURANT
    mid, west_v, east_v = edge_rows(state_ref, west_ref, east_ref, wide, first, step)
    out_ref[:cols, :] = mid
    out_ref[cols:cols + 1, :] = west_v
    out_ref[cols + 1:cols + 2, :] = east_v


def inner_rows(turn_ref, state_ref, west_ref, east_ref, after_ref, out_ref, wide):
    cols = MEMBERS
    first = turn_ref[6:7, :] > 0.5
    step = HALF_COURANT - (2.0 * HALF_COURANT) * turn_ref[6:7, :]
    spin = jnp.where(first, turn_ref[1:2, :], turn_ref[2:3, :])
    mid, west_v, east_v = edge_rows(state_ref, west_ref, east_ref, wide, first, step)
    h, u, v = (row_of(state_ref, f, first) for f in range(3))
    out_ref[:cols, :] = h
    out_ref[cols:2 * cols, :] = v
    out_ref[2 * cols:3 * cols, :] = v + step * row_of(state_ref, 0, ~first) - spin * u
    out_ref[3 * cols:4 * cols, :] = mid
    out_ref[4 * cols:4 * cols + 1, :] = west_v
    out_ref[4 * cols + 1:4 * cols + 2, :] = east_v


def assimilate(
    turn_ref, state_ref, west_ref, east_ref, early_ref, late_ref, inner_ref, weight_ref,
    sent_ref, anomaly_ref, center_ref, wide,
):
    a = HALF_COURANT
    cols = MEMBERS

    def field(f, r):
        k = 2 * f + r
        return state_ref[k * cols:(k + 1) * cols, :]

    def beside(ref, f, r, c):
        k = (2 * f + r) * 2 + c
        return ref[k:k + 1, :]

    def place(slot, block, low, high):
        wide[slot, 8:8 + cols, :] = block
        wide[slot, 7:8, :] = low
        wide[slot, 8 + cols:9 + cols, :] = high

    def slope(slot):
        return wide[slot, 9:9 + cols, :] - wide[slot, 7:7 + cols, :]

    spin = [turn_ref[1:2, :], turn_ref[2:3, :]]
    h = [field(0, 0), field(0, 1)]
    u = [field(1, 0), field(1, 1)]
    v = [field(2, 0), field(2, 1)]
    for r in range(2):
        place(4 + r, h[r], beside(west_ref, 0, r, 1), beside(east_ref, 0, r, 0))
        place(6 + r, u[r], beside(west_ref, 1, r, 1), beside(east_ref, 1, r, 0))
    even = turn_ref[6:7, :] < 0.5
    outer = [early_ref[k * cols:(k + 1) * cols, :] for k in range(3)] + [late_ref[:cols, :]]
    inner = [inner_ref[k * cols:(k + 1) * cols, :] for k in range(4)]
    outer += [late_ref[cols + k:cols + k + 1, :] for k in range(2)]
    inner += [inner_ref[4 * cols + k:4 * cols + k + 1, :] for k in range(2)]
    south_h, south_v, south_mid_v, south_mid_h, *south_edge = (
        jnp.where(even, o, i) for o, i in zip(outer, inner)
    )
    north_h, north_v, north_mid_v, north_mid_h, *north_edge = (
        jnp.where(even, i, o) for o, i in zip(outer, inner)
    )
    h_below, h_above = [south_h, h[0]], [h[1], north_h]
    v_below, v_above = [south_v, v[0]], [v[1], north_v]
    rate_h, rate_u, rate_v, mid_h, mid_u, mid_v = [], [], [], [], [], []
    for r in range(2):
        rate_h.append(-a * (slope(6 + r) + (v_above[r] - v_below[r])))
        rate_u.append(-a * slope(4 + r) + spin[r] * v[r])
        rate_v.append(-a * (h_above[r] - h_below[r]) - spin[r] * u[r])
        mid_h.append(h[r] + rate_h[r])
        mid_u.append(u[r] + rate_u[r])
        mid_v.append(v[r] + rate_v[r])
    for r in range(2):
        outside_h, outside_u = [], []
        for side, ref in enumerate((west_ref, east_ref)):
            near, far = (1, 0) if side == 0 else (0, 1)
            inner_h = h[r][0:1, :] if side == 0 else h[r][cols - 1:cols, :]
            inner_u = u[r][0:1, :] if side == 0 else u[r][cols - 1:cols, :]
            sign = -a if side == 0 else a
            own = [beside(ref, 2, 0, near), beside(ref, 2, 1, near)]
            below = south_edge[side] if r == 0 else own[0]
            above = own[1] if r == 0 else north_edge[side]
            outside_h.append(
                beside(ref, 0, r, near) + sign * (inner_u - beside(ref, 1, r, far)) - a * (above - below)
            )
            outside_u.append(
                beside(ref, 1, r, near) + sign * (inner_h - beside(ref, 0, r, far)) + spin[r] * own[r]
            )
        place(r, mid_h[r], *outside_h)
        place(2 + r, mid_u[r], *outside_u)
    has_south, has_north = turn_ref[4:5, :], turn_ref[5:6, :]
    south_mid_h = has_south * (south_mid_h - a * v[0])
    south_mid_v = has_south * (south_mid_v - a * h[0])
    north_mid_h = has_north * (north_mid_h + a * v[1])
    north_mid_v = has_north * (north_mid_v + a * h[1])
    mid_h_below, mid_h_above = [south_mid_h, mid_h[0]], [mid_h[1], north_mid_h]
    mid_v_below, mid_v_above = [south_mid_v, mid_v[0]], [mid_v[1], north_mid_v]
    forecast = [None] * 6
    for r in range(2):
        second_h = -a * (slope(2 + r) + (mid_v_above[r] - mid_v_below[r]))
        second_u = -a * slope(r) + spin[r] * mid_v[r]
        second_v = -a * (mid_h_above[r] - mid_h_below[r]) - spin[r] * mid_u[r]
        forecast[r] = h[r] + 0.5 * (rate_h[r] + second_h)
        forecast[2 + r] = u[r] + 0.5 * (rate_u[r] + second_u)
        forecast[4 + r] = v[r] + 0.5 * (rate_v[r] + second_v)
    share = jnp.full((8, MEMBERS), 1.0 / MEMBERS, jnp.float32)
    push = jnp.zeros((1, MEMBERS), jnp.float32)
    anomalies, weighted = [], []
    for k in range(6):
        mean = jnp.sum(forecast[k], axis=1, keepdims=True) * (1.0 / MEMBERS)
        anomaly = forecast[k] - mean
        anomaly_ref[k * cols:(k + 1) * cols, :] = anomaly
        row = lax.dot_general(
            share, forecast[k], (((1,), (1,)), ((), ())), precision=lax.Precision.HIGHEST,
            preferred_element_type=jnp.float32,
        )
        center_ref[k:k + 1, :] = row[0:1, :]
        weight = weight_ref[k * cols:(k + 1) * cols, 0:1]
        pull = weight_ref[k * cols:(k + 1) * cols, 1:2] - weight * mean
        push = push + jnp.sum(pull * anomaly, axis=0, keepdims=True)
        anomalies.append(anomaly)
        weighted.append(weight * anomaly)
    gram = lax.dot_general(
        jnp.concatenate(weighted, axis=0), jnp.concatenate(anomalies, axis=0), (((0,), (0,)), ((), ())),
        precision=lax.Precision.HIGHEST, preferred_element_type=jnp.float32,
    )
    row_at = lax.broadcasted_iota(jnp.int32, (MEMBERS, MEMBERS), 0)
    col_at = lax.broadcasted_iota(jnp.int32, (MEMBERS, MEMBERS), 1)
    sent = jnp.where((row_at == MEMBERS - 1) & (col_at < MEMBERS - 1), push, gram)
    sent_ref[...] = jnp.where((row_at == MEMBERS - 2) & (col_at == 0), push[:, MEMBERS - 1:], sent)


def shards(prior_ensemble, observed, obs_error, obs_index, obs_count):
    a = HALF_COURANT
    members, rows, cols = prior_ensemble.shape[1:]
    entries = 3 * rows * cols
    lat_index, lon_index = lax.axis_index(LAT), lax.axis_index(LON)
    lat_count, lon_count = lax.axis_size(LAT), lax.axis_size(LON)
    lat_perms = pair_perms(lat_count, False)
    lon_perms = pair_perms(lon_count, True)
    lat_even, lon_even = lax.rem(lat_index, 2) == 0, lax.rem(lon_index, 2) == 0
    total_rows = rows * lat_count
    turn = rotation_at(lat_index * rows - 1 + jnp.arange(4, dtype=jnp.int32), total_rows)
    has_south = (lat_index > 0).astype(jnp.float32)
    has_north = (lat_index < lat_count - 1).astype(jnp.float32)

    vmem = pl.BlockSpec(memory_space=pltpu.VMEM)
    params = pltpu.CompilerParams(vmem_limit_bytes=16 * 1024 * 1024)
    small = pl.CostEstimate(flops=10**5, bytes_accessed=10**5, transcendentals=0)
    edges = 2 * 3 * rows

    def shaped(*heights):
        return [jax.ShapeDtypeStruct((height, members), jnp.float32) for height in heights]

    lon_flag = jnp.broadcast_to(lon_even.astype(jnp.float32), (8, members))
    state, outer_edge = pl.pallas_call(
        turned,
        in_specs=[vmem] * 2,
        out_specs=[vmem] * 2,
        out_shape=shaped(entries, edges),
        scratch_shapes=[pltpu.VMEM((rows * members, cols), jnp.float32)],
        compiler_params=params,
        cost_estimate=small,
    )(lon_flag, prior_ensemble.reshape(entries, cols))
    lon_inner, lon_outer = lon_perms
    outer_edge = lax.ppermute(outer_edge, LON, lon_outer)

    inner_perm, outer_perm = lat_perms
    edge_row = 1.0 - lat_even.astype(jnp.float32)
    scalars = jnp.concatenate([turn, jnp.stack([has_south, has_north, edge_row, edge_row])])
    scalars = jnp.broadcast_to(scalars[:, None], (8, members))
    early = pl.pallas_call(
        early_rows, in_specs=[vmem] * 2, out_specs=vmem, out_shape=shaped(3 * cols)[0],
        compiler_params=params, cost_estimate=small,
    )(scalars, state)
    outer_early = lax.ppermute(early, LAT, outer_perm)

    inner_edge = pl.pallas_call(
        inner_edges, in_specs=[vmem] * 3, out_specs=vmem, out_shape=shaped(edges)[0],
        compiler_params=params, cost_estimate=small,
    )(lon_flag, state, early)
    inner_edge = lax.ppermute(inner_edge, LON, lon_inner)
    inner_edge, _ = lax.optimization_barrier((inner_edge, early))
    west = jnp.where(lon_even, outer_edge, inner_edge)
    east = jnp.where(lon_even, inner_edge, outer_edge)

    wide_row = [pltpu.VMEM((cols + 16, members), jnp.float32)]
    late = pl.pallas_call(
        late_rows, in_specs=[vmem] * 4, out_specs=vmem, out_shape=shaped(cols + 2)[0],
        scratch_shapes=wide_row, compiler_params=params, cost_estimate=small,
    )(scalars, state, west, east)
    outer_late = lax.ppermute(late, LAT, outer_perm)
    inner = pl.pallas_call(
        inner_rows, in_specs=[vmem] * 5, out_specs=vmem, out_shape=shaped(4 * cols + 2)[0],
        scratch_shapes=wide_row, compiler_params=params, cost_estimate=small,
    )(scalars, state, west, east, late)
    inner = lax.ppermute(inner, LAT, inner_perm)

    index = obs_index.reshape(-1)
    slots = index.shape[0]
    live = (jnp.arange(slots, dtype=jnp.int32) < obs_count.reshape(())).astype(jnp.float32)
    weight = live / obs_error.reshape(-1)
    weight = weight * weight
    named = (jnp.arange(entries, dtype=jnp.int32)[:, None] == index[None, :]).astype(jnp.float32)
    weights = jnp.dot(
        named, jnp.stack([weight, weight * observed.reshape(-1)], axis=1), precision=lax.Precision.HIGHEST
    )
    sent, anomaly, center = pl.pallas_call(
        assimilate,
        in_specs=[vmem] * 8,
        out_specs=[vmem] * 3,
        out_shape=[
            jax.ShapeDtypeStruct((members, members), jnp.float32),
            jax.ShapeDtypeStruct((entries, members), jnp.float32),
            jax.ShapeDtypeStruct((3 * rows, cols), jnp.float32),
        ],
        scratch_shapes=[pltpu.VMEM((8, cols + 16, members), jnp.float32)],
        compiler_params=params,
        cost_estimate=pl.CostEstimate(flops=3 * 10**7, bytes_accessed=2 * 10**6, transcendentals=0),
    )(
        scalars, state, west, east, outer_early, outer_late, inner, weights,
    )
    total = all_sum(sent)
    posterior = pl.pallas_call(
        finish,
        out_shape=jax.ShapeDtypeStruct((entries, cols), jnp.float32),
        scratch_shapes=[pltpu.VMEM((members, 2 * members), jnp.float32)],
        compiler_params=params,
        cost_estimate=pl.CostEstimate(flops=3 * 10**7, bytes_accessed=10**6, transcendentals=0),
    )(total, anomaly, center)
    return posterior.reshape(3, members, rows, cols)


def solution(mesh):
    lat, lon = mesh.shape["lat"], mesh.shape["lon"]
    parts = Mesh(mesh.devices.reshape(lat // 4, 2, 2, lon // 4, 4), LAT + LON)
    placed = (
        P(None, None, LAT, LON),
        P(LAT, LON, None),
        P(LAT, LON, None),
        P(LAT, LON, None),
        P(LAT, LON),
    )
    return jax.shard_map(
        shards, mesh=parts, in_specs=placed, out_specs=P(None, None, LAT, LON), check_vma=False
    )
```
